32 devices in a mesh: ctx: 8 (over y, x, core), tp: 4 (over z).
Axes of the slice: x: 2, y: 2, z: 4, core: 2. Of those that a mesh axis runs over, the one named last changes fastest.
Arguments:
- queries: bfloat16 [12288, 4096], P('ctx', 'tp'), may hold values from -6 to 6
- keys: bfloat16 [12288, 4096], P('ctx', 'tp'), may hold values from -6 to 6
- values: bfloat16 [12288, 4096], P('ctx', 'tp'), may hold values from -51 to 51, as said below
- out_grad: bfloat16 [12288, 4096], P('ctx', 'tp'), may hold values from -6 to 6
- gain: float32 [4096], P('tp'), may hold values from 0.25 to 1.75
- doc_ids: int32 [48], P('ctx'), may hold values from 0 to 7, never falling along the last dimension, each value on 1 to 24 neighbouring positions
Outputs:
- normed: bfloat16 [12288, 4096], P('ctx', 'tp')
- query_grad: bfloat16 [12288, 4096], P('ctx', 'tp')
- key_grad: bfloat16 [12288, 4096], P('ctx', 'tp')
- value_grad: bfloat16 [12288, 4096], P('ctx', 'tp')
The draws below stay inside these ranges and needn't reach their ends.
Inputs may be any that keep to these rules, and one draw needn't show every extreme that they name: `doc_ids`: never falls along the sequence; each document covers 1 to max(4, 24) blocks, and one covers exactly that many. `values`: values of order one to ten, with scales that differ from token to token and from feature to feature.
All inputs are finite; a program needn't handle non-finite values.
Results may differ from the reference program's by a relative error of at most 0.0058.
Values sent between devices are 32-bit elements; how exact they have to be, the bound alone decides.
No kernel may reach another device: no remote copies, remote signals or barrier semaphores. Data moves between devices by JAX's collectives and lax.ppermute only.
A program may use at most 128 MiB of HBM per device.

```python
import math
import jax
import jax.numpy as jnp
import numpy as np
from jax import lax

H = 32
HD = 128
C = 256
TOKENS = 12288
NCH = 48
QW = 4096


def draw_values(key, part):
    first_key, second_key, third_key = jax.random.split(key, 3)
    columns = jnp.arange(QW)
    head_index = (columns // HD).astype(jnp.float32)
    head_rise = head_index / max(H - 1, 1)
    noise_part = jnp.clip(jax.random.normal(first_key, (TOKENS, QW), jnp.float32), -4.0, 4.0)
    head_level = 3.0 ** (head_rise - 1.0)
    column_scale = jnp.exp(jax.random.uniform(second_key, (QW,), jnp.float32, 0.0, math.log(4.0)))
    row_scale = jnp.exp(jax.random.uniform(third_key, (TOKENS, 1), jnp.float32, -1.15, 1.15))
    return (noise_part * (head_level * column_scale)[None, :] * row_scale).astype(jnp.bfloat16)


def block_scale(key, extent, cuts, low, largest):
    loudness = 1.0
    for dim, parts in cuts:
        steps = jax.random.uniform(jax.random.fold_in(jax.random.fold_in(key, 6), dim), (parts,), jnp.float32, low / len(cuts), largest / len(cuts))
        loudness = loudness * jnp.repeat(jnp.exp(steps), extent[dim] // parts).reshape((-1,) + (1,) * (len(extent) - 1 - dim))
    return loudness


def length_profile(amount, total, bound, skew):
    weights = [(1 << 20) // math.isqrt(grade ** skew) + 1 for grade in range(2, amount + 1)]
    spare, counts = total - bound - (amount - 1), [1] * (amount - 1)
    while spare > 0:
        candidates = [i for i in range(amount - 1) if counts[i] < bound]
        mass, budget = sum([weights[i] for i in candidates]), spare
        for i in candidates:
            more = min(bound - counts[i], max(1, budget * weights[i] // mass), spare)
            counts[i] = counts[i] + more
            spare = spare - more
    return np.array([bound] + counts)


def uneven(own_key, number_of, total, bound, skew):
    if number_of == 2:
        one = jax.random.randint(own_key, (), max(1, total - bound), min(bound, total - 1) + 1)
        return jnp.stack([one, total - one])
    tallies = jnp.asarray(length_profile(number_of, total, bound, skew), jnp.int32)
    pairs = (number_of - 1) // 2
    giver, receiver = tallies[1:1 + 2 * pairs:2], tallies[2:2 + 2 * pairs:2]
    room = jnp.minimum(giver - 1, bound - receiver)
    shifted = jax.random.randint(jax.random.fold_in(own_key, 1), (pairs,), 0, 1 << 20) % (room + 1)
    tallies = tallies.at[1:1 + 2 * pairs:2].set(giver - shifted).at[2:2 + 2 * pairs:2].set(receiver + shifted)
    return tallies[jax.random.permutation(jax.random.fold_in(own_key, 2), number_of)]


def normal_values(stream_key, dims, spread, bound, shards=(), held_as=jnp.bfloat16):
    values = jax.random.normal(stream_key, dims, jnp.float32) * spread
    if len(shards) > 0:
        values = block_scale(stream_key, dims, shards, -0.22, 0.18) * values
    return jnp.clip(values, min=-bound, max=bound).astype(held_as)


def setup_inputs(seed: int = 0) -> dict:
    splits = jax.random.split(jax.random.key(seed), 7)
    return {
        "queries": normal_values(splits[0], (TOKENS, QW), 1.0, 6.0, ((0, 8), (1, 4))),
        "keys": normal_values(splits[1], (TOKENS, QW), 1.0, 6.0, ((0, 8), (1, 4))),
        "values": draw_values(jax.random.fold_in(splits[6], 71), 0),
        "out_grad": normal_values(splits[3], (TOKENS, QW), 1.0, 6.0, ((0, 8), (1, 4))),
        "gain": jnp.clip(1.0 + 0.15 * jax.random.normal(splits[4], (QW,), jnp.float32), 0.25, 1.75),
        "doc_ids": jnp.searchsorted(jnp.cumsum(uneven(splits[5], max(3, NCH // 6), NCH, max(4, NCH // 2), 1)), jnp.arange(NCH), side="right").astype(jnp.int32),
    }


epsilon = 1e-06

def to_low(array):
    return lax.optimization_barrier(array.astype(jnp.bfloat16)).astype(jnp.float32)

def reference(queries, keys, values, out_grad, gain, doc_ids):
    query_blk = queries.reshape(NCH, C, H, HD)
    key_blk = keys.reshape(NCH, C, H, HD)
    value_blk = values.reshape(NCH, C, H, HD)
    grad_blk = out_grad.reshape(NCH, C, QW)
    doc_of = doc_ids.astype(jnp.int32)
    earlier_doc = jnp.concatenate([jnp.full((1,), -1, jnp.int32), doc_of[:-1]])
    later_doc = jnp.concatenate([doc_of[1:], jnp.full((1,), -1, jnp.int32)])
    starts = doc_of != earlier_doc
    finals = doc_of != later_doc
    causal = jnp.tril(jnp.ones((C, C), dtype=bool))
    gain32 = gain.astype(jnp.float32)

    def forward(carried, pieces):
        query_c, key_c, value_c, grad_c, opens = pieces
        carried = jnp.where(opens, jnp.zeros_like(carried), carried)
        state_low = to_low(carried)
        query_f = query_c.astype(jnp.float32)
        key_f = key_c.astype(jnp.float32)
        value_f = value_c.astype(jnp.float32)
        scores = jnp.einsum('thd,shd->hts', query_f, key_f)
        scores = to_low(jnp.where(causal[None], scores, 0.0))
        attended = jnp.einsum('thd,hde->the', query_f, state_low) + jnp.einsum('hts,she->the', scores, value_f)
        flat_out = attended.reshape(C, QW)
        total_sq = lax.optimization_barrier(jnp.sum(flat_out * flat_out, axis=1, keepdims=True))
        scale_inv = lax.rsqrt(total_sq / QW + epsilon)
        normed = (flat_out * scale_inv * gain32).astype(jnp.bfloat16)
        weighted = grad_c.astype(jnp.float32) * gain32
        inner_sum = lax.optimization_barrier(jnp.sum(weighted * flat_out, axis=1, keepdims=True))
        mixed_grad = scale_inv * weighted - flat_out * scale_inv ** 3 * (inner_sum / QW)
        grad_low = mixed_grad.astype(jnp.bfloat16)
        grad_f = lax.optimization_barrier(grad_low).astype(jnp.float32).reshape(C, H, HD)
        grad_scores = to_low(jnp.where(causal[None], jnp.einsum('the,she->hts', grad_f, value_f), 0.0))
        query_grad = jnp.einsum('the,hde->thd', grad_f, state_low) + jnp.einsum('hts,shd->thd', grad_scores, key_f)
        carried = carried + jnp.einsum('shd,she->hde', key_f, value_f)
        return (carried, (normed, grad_low, query_grad.astype(jnp.bfloat16).reshape(C, QW)))
    start_state = jnp.zeros((H, HD, HD), jnp.float32)
    _, (normed, grad_low, query_grad) = lax.scan(forward, start_state, (query_blk, key_blk, value_blk, grad_blk, starts))

    def backward(carried, pieces):
        query_c, key_c, value_c, grad_c, closes = pieces
        carried = jnp.where(closes, jnp.zeros_like(carried), carried)
        state_low = to_low(carried)
        query_f = query_c.astype(jnp.float32)
        key_f = key_c.astype(jnp.float32)
        value_f = value_c.astype(jnp.float32)
        grad_f = grad_c.astype(jnp.float32).reshape(C, H, HD)
        scores = to_low(jnp.where(causal[None], jnp.einsum('thd,shd->hts', query_f, key_f), 0.0))
        grad_scores = to_low(jnp.where(causal[None], jnp.einsum('the,she->hts', grad_f, value_f), 0.0))
        key_grad = jnp.einsum('she,hde->shd', value_f, state_low) + jnp.einsum('hts,thd->shd', grad_scores, query_f)
        value_grad = jnp.einsum('shd,hde->she', key_f, state_low) + jnp.einsum('hts,the->she', scores, grad_f)
        carried = carried + jnp.einsum('thd,the->hde', query_f, grad_f)
        return (carried, (key_grad.astype(jnp.bfloat16).reshape(C, QW), value_grad.astype(jnp.bfloat16).reshape(C, QW)))
    _, (key_grad, value_grad) = lax.scan(backward, start_state, (query_blk, key_blk, value_blk, grad_low, finals), reverse=True)
    return (normed.reshape(TOKENS, QW), query_grad.reshape(TOKENS, QW), key_grad.reshape(TOKENS, QW), value_grad.reshape(TOKENS, QW))
```

```python
import functools

import jax
import jax.numpy as jnp
from jax import lax
from jax.experimental import pallas as pl
from jax.experimental.pallas import tpu as pltpu
from jax.sharding import PartitionSpec as P

HD = 128
C = 256
QW = 4096
PAD = 8
NEVER = -1.0e9
MIB = 1 << 20

epsilon = 1e-06

F32 = jnp.float32
BF16 = jnp.bfloat16
VM = pl.BlockSpec(memory_space=pltpu.VMEM)
SM = pl.BlockSpec(memory_space=pltpu.SMEM)
ANY = pl.BlockSpec(memory_space=pl.ANY)
HB = pl.BlockSpec(memory_space=pltpu.HBM)


def dot(a, b, dims):
    return lax.dot_general(a, b, (dims, ((), ())), preferred_element_type=F32)


NN = ((1,), (0,))
NT = ((1,), (1,))
TN = ((0,), (0,))


def params(mib=12):
    return pltpu.CompilerParams(vmem_limit_bytes=mib * MIB)


def cost(flops, nbytes):
    return pl.CostEstimate(flops=int(flops), bytes_accessed=int(nbytes), transcendentals=0)


def half_start(own, cols):
    core = lax.rem(lax.axis_index("ctx"), 2)
    half = core if own else 1 - core
    return pl.multiple_of(half * cols, 128)


def head(h):
    return pl.ds(h * HD, HD)


def block(n):
    return pl.ds(pl.multiple_of(n * C, C), C)


def state_rows(n, h, heads):
    return pl.ds(pl.multiple_of((n * heads + h) * HD, HD), HD)


def key_value_states(own, blocks, heads, docs, k_hbm, v_hbm, k, v, inside, message, sems):
    off = half_start(own, heads * HD)
    copies = []
    for h in range(heads):
        src = pl.ds(off + h * HD, HD)
        pair = (
            pltpu.make_async_copy(k_hbm.at[:, src], k.at[:, head(h)], sems.at[2 * h]),
            pltpu.make_async_copy(v_hbm.at[:, src], v.at[:, head(h)], sems.at[2 * h + 1]),
        )
        for copy in pair:
            copy.start()
        copies.append(pair)
    for h in range(heads):
        for copy in copies[h]:
            copy.wait()
        running = jnp.zeros((HD, HD), F32)
        for n in range(blocks):
            inside[state_rows(n, h, heads), :] = running
            rows = pl.ds(n * C, C)
            total = running + dot(k[rows, head(h)], v[rows, head(h)], TN)
            if n + 1 < blocks:
                running = jnp.where(docs[n] == docs[n + 1], total, 0.0)
            else:
                message[head(h), :] = total
    message[heads * HD :, :] = jnp.full((PAD, HD), docs[blocks - 1].astype(F32), F32)


def local_scores(own, blocks, heads, k, v, q_hbm, g_hbm, q, g, local, scores, sems, gsem):
    off = half_start(own, heads * HD)
    cols = pl.ds(off, heads * HD)

    def q_copy(n):
        return pltpu.make_async_copy(q_hbm.at[block(n), cols], q.at[block(n), :], sems.at[n])

    for n in range(blocks):
        q_copy(n).start()
    g_copy = pltpu.make_async_copy(g_hbm.at[:, cols], g, gsem)
    g_copy.start()
    causal = lax.broadcasted_iota(jnp.int32, (C, C), 0) >= lax.broadcasted_iota(
        jnp.int32, (C, C), 1
    )

    def step(n, carry):
        q_copy(n).wait()
        rows = block(n)
        for h in range(heads):
            s = dot(q[rows, head(h)], k[rows, head(h)], NT)
            s = jnp.where(causal, s, 0.0).astype(BF16)
            scores[pl.ds(pl.multiple_of((n * heads + h) * C, C), C), :] = s
            local[rows, head(h)] = dot(s, v[rows, head(h)], NN)
        return carry

    lax.fori_loop(0, blocks, step, 0)
    g_copy.wait()


def attend(own, blocks, heads, lanes, docs, inside, carry, q, local, g, gain, *rest):
    if own:
        attended, low, sums = rest
        sums[...] = jnp.zeros((C, HD), F32)
    else:
        sums_in, attended, low, message, sums = rest
        sums[...] = sums_in[...]
    off = half_start(own, heads * HD)
    gains = gain[:, pl.ds(off, heads * HD)]
    lane = lax.broadcasted_iota(jnp.int32, (C, HD), 1)

    def step(n, carried):
        rows = block(n)
        hit = carry[heads * HD : heads * HD + 1, :] == docs[n].astype(F32)
        square = jnp.zeros((C, HD), F32)
        inner = jnp.zeros((C, HD), F32)
        for h in range(heads):
            here = state_rows(n, h, heads)
            state = inside[here, :] + jnp.where(hit, carry[head(h), :], 0.0)
            state_low = state.astype(BF16)
            low[here, :] = state_low
            out = local[rows, head(h)] + dot(q[rows, head(h)], state_low, NN)
            attended[rows, head(h)] = out
            weighted = g[rows, head(h)].astype(F32) * gains[:, h * HD : (h + 1) * HD]
            square += out * out
            inner += weighted * out
        square = jnp.sum(square, axis=1, keepdims=True)
        inner = jnp.sum(inner, axis=1, keepdims=True)
        sums[...] += jnp.where(lane == n, square, 0.0) + jnp.where(lane == n + lanes, inner, 0.0)
        return carried

    lax.fori_loop(0, blocks, step, 0)
    if not own:
        message[...] = jnp.transpose(sums[...])[: 2 * lanes, :]


def mixed(own, blocks, heads, lanes, parts, docs, *rest):
    if not own:
        pieces, rest = rest[:parts], rest[parts:]
        attended, q, g, gain, grad, inside, message, scale, slope, running, turn = rest
        total = pieces[0][...]
        for piece in pieces[1:]:
            total = total + piece[...]
        r = lax.rsqrt(total[:lanes] / QW + epsilon)
        s = r * r * r * (total[lanes:] / QW)
        turn[...] = jnp.zeros((HD, C), F32)
        turn[:lanes, :] = r
        turn[lanes : 2 * lanes, :] = s
        columns = jnp.transpose(turn[...])
        for n in range(blocks):
            rows = pl.ds(n * C, C)
            scale[rows, :] = jnp.broadcast_to(columns[:, n : n + 1], (C, HD))
            slope[rows, :] = jnp.broadcast_to(columns[:, lanes + n : lanes + n + 1], (C, HD))
    else:
        scale, slope, attended, q, g, gain, grad, inside, message, running = rest
    off = half_start(own, heads * HD)
    gains = gain[:, pl.ds(off, heads * HD)]
    running[...] = jnp.zeros((heads * HD, HD), F32)

    def step(i, carried):
        n = blocks - 1 - i
        rows = block(n)
        linked = docs[n] == docs[jnp.maximum(n - 1, 0)]
        r = scale[rows, :]
        s = slope[rows, :]
        for h in range(heads):
            weighted = g[rows, head(h)].astype(F32) * gains[:, h * HD : (h + 1) * HD]
            d = (r * weighted - attended[rows, head(h)] * s).astype(BF16)
            grad[rows, head(h)] = d
            state = running[head(h), :]
            inside[state_rows(n, h, heads), :] = state
            state = state + dot(q[rows, head(h)], d, TN)
            message[head(h), :] = state
            running[head(h), :] = jnp.where(linked, state, 0.0)
        return carried

    lax.fori_loop(0, blocks, step, 0)
    message[heads * HD :, :] = jnp.full((PAD, HD), -docs[0].astype(F32), F32)


def store_blocks(n, pairs, cols, sems):
    slot = lax.rem(n, 2)
    return [
        pltpu.make_async_copy(stage.at[slot], out.at[block(n), cols], sems.at[i, slot])
        for i, (stage, out) in enumerate(pairs)
    ]


def query_side(own, blocks, heads, k, v, q, attended, scale, gain, grad, low, scores, *rest):
    if not own:
        normed, query_grad, key_local, value_local, stage_n, stage_q, sems = rest
    else:
        _, _, normed, query_grad, key_local, value_local, stage_n, stage_q, sems = rest
    off = half_start(own, heads * HD)
    cols = pl.ds(off, heads * HD)
    gains = gain[:, cols]
    pairs = ((stage_n, normed), (stage_q, query_grad))
    causal = lax.broadcasted_iota(jnp.int32, (C, C), 0) >= lax.broadcasted_iota(
        jnp.int32, (C, C), 1
    )

    def step(n, carried):
        rows = block(n)
        slot = lax.rem(n, 2)

        @pl.when(n >= 2)
        def _():
            for copy in store_blocks(n - 2, pairs, cols, sems):
                copy.wait()

        r = scale[rows, :]
        for h in range(heads):
            d = grad[rows, head(h)]
            gs = dot(d, v[rows, head(h)], NT)
            gs = jnp.where(causal, gs, 0.0).astype(BF16)
            qg = dot(d, low[state_rows(n, h, heads), :], NT) + dot(gs, k[rows, head(h)], NN)
            stage_q[slot, :, head(h)] = qg.astype(BF16)
            key_local[rows, head(h)] = dot(gs, q[rows, head(h)], TN)
            s = scores[pl.ds(pl.multiple_of((n * heads + h) * C, C), C), :]
            value_local[rows, head(h)] = dot(s, d, TN)
            out = attended[rows, head(h)] * r * gains[:, h * HD : (h + 1) * HD]
            stage_n[slot, :, head(h)] = out.astype(BF16)
        for copy in store_blocks(n, pairs, cols, sems):
            copy.start()
        return carried

    lax.fori_loop(0, blocks, step, 0)
    for n in range(max(blocks - 2, 0), blocks):
        for copy in store_blocks(n, pairs, cols, sems):
            copy.wait()


def key_side(own, blocks, heads, docs, inside, carry, k, v, key_local, value_local, *rest):
    if own:
        key_grad, value_grad, stage_k, stage_v, sems = rest
    else:
        _, _, key_grad, value_grad, stage_k, stage_v, sems = rest
    off = half_start(own, heads * HD)
    cols = pl.ds(off, heads * HD)
    pairs = ((stage_k, key_grad), (stage_v, value_grad))

    def step(n, carried):
        rows = block(n)
        slot = lax.rem(n, 2)

        @pl.when(n >= 2)
        def _():
            for copy in store_blocks(n - 2, pairs, cols, sems):
                copy.wait()

        hit = carry[heads * HD : heads * HD + 1, :] == -docs[n].astype(F32)
        for h in range(heads):
            state = inside[state_rows(n, h, heads), :] + jnp.where(hit, carry[head(h), :], 0.0)
            leave = state.astype(BF16)
            kg = key_local[rows, head(h)] + dot(v[rows, head(h)], leave, NT)
            vg = value_local[rows, head(h)] + dot(k[rows, head(h)], leave, NN)
            stage_k[slot, :, head(h)] = kg.astype(BF16)
            stage_v[slot, :, head(h)] = vg.astype(BF16)
        for copy in store_blocks(n, pairs, cols, sems):
            copy.start()
        return carried

    lax.fori_loop(0, blocks, step, 0)
    for n in range(max(blocks - 2, 0), blocks):
        for copy in store_blocks(n, pairs, cols, sems):
            copy.wait()


def merge_kernel(reverse, outs, count, *refs):
    size = lax.axis_size("ctx")
    rank = lax.axis_index("ctx")
    if reverse:
        rank = size - 1 - rank

    def bit(b):
        return lax.rem(lax.div(rank, 1 << b), 2)

    ins, results = refs[:count], refs[count:]
    for pieces, result in zip(outs, results):
        at = 0
        latest = None
        for rows, terms in pieces:
            keys = []
            for source, start, flag in terms:
                last = ins[source].shape[0] - PAD
                key = ins[source][last : last + 1, :]
                keys.append(key if flag is None else jnp.where(flag(bit), key, NEVER))
            latest = functools.reduce(jnp.maximum, keys)
            value = None
            for (source, start, _), key in zip(terms, keys):
                part = jnp.where(key == latest, ins[source][start : start + rows, :], 0.0)
                value = part if value is None else value + part
            result[at : at + rows, :] = value
            at += rows
        result[at:, :] = jnp.broadcast_to(latest, (PAD, HD))


def merge(ins, outs, reverse):
    shapes = [pltpu.VMEM((sum(rows for rows, _ in pieces) + PAD, HD), F32) for pieces in outs]
    return pl.pallas_call(
        functools.partial(merge_kernel, reverse, outs, len(ins)),
        out_shape=shapes,
        in_specs=[VM] * len(ins),
        out_specs=[VM] * len(outs),
        compiler_params=params(),
        cost_estimate=cost(0, 1 << 18),
    )(*ins)


def swap(message, b):
    size = lax.axis_size("ctx")
    return lax.ppermute(message, "ctx", [(i, i ^ (1 << b)) for i in range(size)])


def scan(theirs, mine, reverse):
    rows = mine.shape[0] - PAD
    part = rows // 2
    top = lax.axis_size("ctx").bit_length() - 1
    lo, hi = top - 2, top - 1
    beside = swap(theirs, 0)
    halves = [[(part, [(0, start, None), (1, start, None)])] for start in (0, part)]
    total_a, total_b = merge([mine, beside], halves, reverse)
    before_a, before_b = [], []
    for b in range(1, lo):
        got_a, got_b = swap(total_a, b), swap(total_b, b)

        def is_high(bit, b=b):
            return bit(b) == 1

        ins = [total_a, total_b, got_a, got_b] + before_a + before_b
        earlier_a = [(4, 0, None)] if before_a else []
        earlier_b = [(5, 0, None)] if before_b else []
        total_a, total_b, pa, pb = merge(
            ins,
            [
                [(part, [(0, 0, None), (2, 0, None)])],
                [(part, [(1, 0, None), (3, 0, None)])],
                [(part, [(2, 0, is_high)] + earlier_a)],
                [(part, [(3, 0, is_high)] + earlier_b)],
            ],
            reverse,
        )
        before_a, before_b = [pa], [pb]
    first_a, first_b = swap(total_a, lo), swap(total_b, hi)
    next_a, next_b = merge(
        [total_a, first_a, total_b, first_b],
        [
            [(part, [(0, 0, None), (1, 0, None)])],
            [
                (
                    part,
                    [
                        (2, 0, lambda bit: bit(lo) * bit(hi) == 0),
                        (3, 0, lambda bit: bit(hi) == 1),
                    ],
                )
            ],
        ],
        reverse,
    )
    second_a, second_b = swap(next_a, hi), swap(next_b, lo)

    def carried(neighbour, flag):
        terms_a = [(0, 0, lambda bit: bit(lo) == 1), (1, 0, lambda bit: bit(hi) == 1)]
        terms_b = [(2, 0, lambda bit: bit(hi) == 1), (3, 0, lambda bit: bit(lo) + bit(hi) > 0)]
        if before_a:
            terms_a.append((6, 0, None))
            terms_b.append((7, 0, None))
        return [
            (part, terms_a + [(neighbour, 0, flag)]),
            (part, terms_b + [(neighbour, part, flag)]),
        ]

    carry_mine, carry_theirs = merge(
        [first_a, second_a, first_b, second_b, beside, mine] + before_a + before_b,
        [carried(4, lambda bit: bit(0) == 1), carried(5, lambda bit: bit(0) == 0)],
        reverse,
    )
    return carry_mine, swap(carry_theirs, 0)


def local(queries, keys, values, out_grad, gain, doc_ids):
    tokens, features = queries.shape
    heads = features // HD // 2
    cols = heads * HD
    blocks = tokens // C
    lanes = -(-blocks // 8) * 8
    pairs = blocks * heads
    tp = lax.axis_size("tp")
    gain = gain.reshape(1, features)
    rows = cols + PAD
    narrow, wide, square = C * HD * HD, C * C * HD, HD * HD
    dma = pltpu.SemaphoreType.DMA
    half_bf = pltpu.VMEM((tokens, cols), BF16)
    half_f32 = pltpu.VMEM((tokens, cols), F32)
    states_f32 = pltpu.VMEM((pairs * HD, HD), F32)
    message = pltpu.VMEM((rows, HD), F32)
    whole = pltpu.HBM((tokens, features), BF16)
    column = pltpu.VMEM((tokens, HD), F32)

    def states(own):
        return pl.pallas_call(
            functools.partial(key_value_states, own, blocks, heads),
            out_shape=[half_bf, half_bf, states_f32, message],
            in_specs=[SM, ANY, ANY],
            out_specs=[VM] * 4,
            scratch_shapes=[dma((2 * heads,))],
            compiler_params=params(),
            cost_estimate=cost(2 * pairs * narrow, 4 * tokens * cols),
        )(doc_ids, keys, values)

    def scoring(own, k, v):
        return pl.pallas_call(
            functools.partial(local_scores, own, blocks, heads),
            out_shape=[half_bf, half_bf, half_f32, pltpu.VMEM((pairs * C, C), BF16)],
            in_specs=[VM, VM, ANY, ANY],
            out_specs=[VM] * 4,
            scratch_shapes=[dma((blocks,)), dma],
            compiler_params=params(),
            cost_estimate=cost(4 * pairs * wide, 4 * tokens * cols),
        )(k, v, queries, out_grad)

    def attending(own, inside, carry, q, sv, g, sums):
        ins = [doc_ids, inside, carry, q, sv, g, gain] + ([] if own else [sums])
        last = [pltpu.VMEM((C, HD), F32)] if own else [pltpu.VMEM((2 * lanes, C), F32)]
        return pl.pallas_call(
            functools.partial(attend, own, blocks, heads, lanes),
            out_shape=[half_f32, pltpu.VMEM((pairs * HD, HD), BF16)] + last,
            in_specs=[SM] + [VM] * (len(ins) - 1),
            out_specs=[VM] * 3,
            scratch_shapes=[] if own else [pltpu.VMEM((C, HD), F32)],
            input_output_aliases={4: 0},
            compiler_params=params(),
            cost_estimate=cost(2 * pairs * narrow, 1 << 20),
        )(*ins)

    def mixing(own, before, attended, q, g):
        ins = [doc_ids] + before + [attended, q, g, gain]
        outs = [half_bf, states_f32, message] + ([] if own else [column, column])
        scratch = [pltpu.VMEM((cols, HD), F32)]
        return pl.pallas_call(
            functools.partial(mixed, own, blocks, heads, lanes, tp),
            out_shape=outs,
            in_specs=[SM] + [VM] * (len(ins) - 1),
            out_specs=[VM] * len(outs),
            scratch_shapes=scratch if own else scratch + [pltpu.VMEM((HD, C), F32)],
            compiler_params=params(),
            cost_estimate=cost(2 * pairs * narrow, 1 << 20),
        )(*ins)

    def query_grads(own, k, v, q, attended, scale, grad, low, scores, so_far):
        ins = [k, v, q, attended, scale, gain, grad, low, scores] + list(so_far)
        stage = pltpu.VMEM((2, C, cols), BF16)
        return pl.pallas_call(
            functools.partial(query_side, own, blocks, heads),
            out_shape=[whole, whole, half_f32, half_f32],
            in_specs=[VM] * 9 + [HB] * len(so_far),
            out_specs=[HB, HB, VM, VM],
            scratch_shapes=[stage, stage, dma((2, 2))],
            input_output_aliases={9: 0, 10: 1} if own else {},
            compiler_params=params(),
            cost_estimate=cost(8 * pairs * wide, 4 * tokens * cols),
        )(*ins)

    def key_grads(own, inside, carry, k, v, key_local, value_local, so_far):
        ins = [doc_ids, inside, carry, k, v, key_local, value_local] + list(so_far)
        stage = pltpu.VMEM((2, C, cols), BF16)
        return pl.pallas_call(
            functools.partial(key_side, own, blocks, heads),
            out_shape=[whole, whole],
            in_specs=[SM] + [VM] * 6 + [HB] * len(so_far),
            out_specs=[HB, HB],
            scratch_shapes=[stage, stage, dma((2, 2))],
            input_output_aliases={} if own else {7: 0, 8: 1},
            compiler_params=params(),
            cost_estimate=cost(4 * pairs * narrow, 4 * tokens * cols),
        )(*ins)

    k1, v1, inside1, theirs = states(False)
    k0, v0, inside0, mine = states(True)
    carry0, carry1 = scan(theirs, mine, False)
    q1, g1, local1, scores1 = scoring(False, k1, v1)
    q0, g0, local0, scores0 = scoring(True, k0, v0)
    att0, low0, sums = attending(True, inside0, carry0, q0, local0, g0, None)
    att1, low1, sums = attending(False, inside1, carry1, q1, local1, g1, sums)
    parts = [sums] + [
        lax.ppermute(sums, "tp", [(i, (i + s) % tp) for i in range(tp)]) for s in range(1, tp)
    ]
    grad1, after1, theirs, scale, slope = mixing(False, parts, att1, q1, g1)
    grad0, after0, mine = mixing(True, [scale, slope], att0, q0, g0)
    carry0, carry1 = scan(theirs, mine, True)
    normed, query_grad, kl1, vl1 = query_grads(
        False, k1, v1, q1, att1, scale, grad1, low1, scores1, ()
    )
    normed, query_grad, kl0, vl0 = query_grads(
        True, k0, v0, q0, att0, scale, grad0, low0, scores0, (normed, query_grad)
    )
    key_grad, value_grad = key_grads(True, after0, carry0, k0, v0, kl0, vl0, ())
    key_grad, value_grad = key_grads(
        False, after1, carry1, k1, v1, kl1, vl1, (key_grad, value_grad)
    )
    return normed, query_grad, key_grad, value_grad


def solution(mesh):
    return jax.shard_map(
        local,
        mesh=mesh,
        in_specs=(
            P("ctx", "tp"),
            P("ctx", "tp"),
            P("ctx", "tp"),
            P("ctx", "tp"),
            P("tp"),
            P("ctx"),
        ),
        out_specs=(P("ctx", "tp"), P("ctx", "tp"), P("ctx", "tp"), P("ctx", "tp")),
        check_vma=False,
    )
```

```python
import functools

import jax
import jax.numpy as jnp
from jax import lax
from jax.experimental import pallas as pl
from jax.experimental.pallas import tpu as pltpu
from jax.sharding import PartitionSpec as P

HD = 128
C = 256
QW = 4096
PAD = 8
NEVER = -1.0e9
MIB = 1 << 20
UNROLL = 1

epsilon = 1e-06

F32 = jnp.float32
BF16 = jnp.bfloat16
VM = pl.BlockSpec(memory_space=pltpu.VMEM)
SM = pl.BlockSpec(memory_space=pltpu.SMEM)
ANY = pl.BlockSpec(memory_space=pl.ANY)
HB = pl.BlockSpec(memory_space=pltpu.HBM)


def dot(a, b, dims):
    return lax.dot_general(a, b, (dims, ((), ())), preferred_element_type=F32)


NN = ((1,), (0,))
NT = ((1,), (1,))
TN = ((0,), (0,))


def params(mib=12):
    return pltpu.CompilerParams(vmem_limit_bytes=mib * MIB)


def cost(flops, nbytes):
    return pl.CostEstimate(flops=int(flops), bytes_accessed=int(nbytes), transcendentals=0)


def half_start(own, cols):
    core = lax.rem(lax.axis_index("ctx"), 2)
    half = core if own else 1 - core
    return pl.multiple_of(half * cols, 128)


def label(name, own):
    return name + ("_own" if own else "_other")


def head(h):
    return pl.ds(h * HD, HD)


def block(n):
    return pl.ds(pl.multiple_of(n * C, C), C)


def state_rows(n, h, heads):
    return pl.ds(pl.multiple_of((n * heads + h) * HD, HD), HD)


def key_value_states(own, blocks, heads, docs, k_hbm, v_hbm, k, v, inside, message, sems):
    off = half_start(own, heads * HD)
    copies = []
    for h in range(heads):
        src = pl.ds(off + h * HD, HD)
        pair = (
            pltpu.make_async_copy(k_hbm.at[:, src], k.at[:, head(h)], sems.at[2 * h]),
            pltpu.make_async_copy(v_hbm.at[:, src], v.at[:, head(h)], sems.at[2 * h + 1]),
        )
        for copy in pair:
            copy.start()
        copies.append(pair)
    for h in range(heads):
        for copy in copies[h]:
            copy.wait()
        per_block = [pl.ds(n * C, C) for n in range(blocks)]
        sums = [dot(k[rows, head(h)], v[rows, head(h)], TN) for rows in per_block]
        running = jnp.zeros((HD, HD), F32)
        for n in range(blocks):
            inside[state_rows(n, h, heads), :] = running
            total = running + sums[n]
            if n + 1 < blocks:
                running = jnp.where(docs[n] == docs[n + 1], total, 0.0)
            else:
                message[head(h), :] = total
    message[heads * HD :, :] = jnp.full((PAD, HD), docs[blocks - 1].astype(F32), F32)


def causal_mask():
    return lax.broadcasted_iota(jnp.int32, (C, C), 0) >= lax.broadcasted_iota(jnp.int32, (C, C), 1)


def score_rows(n, h, heads):
    return pl.ds(pl.multiple_of((n * heads + h) * C, C), C)


def local_scores(own, blocks, heads, after, k, v, q, local, scores, done):
    off = half_start(own, heads * HD)
    causal = causal_mask()
    every = range(heads)

    def step(n, carry):
        rows = block(n)
        raw = [dot(q[rows, pl.ds(off + h * HD, HD)], k[rows, head(h)], NT) for h in every]
        low = [jnp.where(causal, s, 0.0).astype(BF16) for s in raw]
        outs = [dot(low[h], v[rows, head(h)], NN) for h in every]
        for h in every:
            scores[score_rows(n, h, heads), :] = low[h]
            local[rows, head(h)] = outs[h]
        return carry

    lax.fori_loop(0, blocks, step, 0, unroll=UNROLL)
    done[...] = jnp.zeros(done.shape, F32)


def attend(own, blocks, heads, lanes, docs, inside, carry, q, local, g, gain, *rest):
    if own:
        attended, low, sums = rest
        sums[...] = jnp.zeros((C, HD), F32)
    else:
        sums_in, attended, low, message, sums = rest
        sums[...] = sums_in[...]
    off = half_start(own, heads * HD)
    gains = gain[:, pl.ds(off, heads * HD)]
    lane = lax.broadcasted_iota(jnp.int32, (C, HD), 1)
    every = range(heads)

    def step(n, carried):
        rows = block(n)
        hit = carry[heads * HD : heads * HD + 1, :] == docs[n].astype(F32)
        states = []
        for h in every:
            state = inside[state_rows(n, h, heads), :] + jnp.where(hit, carry[head(h), :], 0.0)
            states.append(state.astype(BF16))
        outs = [dot(q[rows, pl.ds(off + h * HD, HD)], states[h], NN) for h in every]
        outs = [outs[h] + local[rows, head(h)] for h in every]
        square = functools.reduce(jnp.add, [out * out for out in outs])
        inner = functools.reduce(
            jnp.add,
            [
                g[rows, pl.ds(off + h * HD, HD)].astype(F32)
                * gains[:, h * HD : (h + 1) * HD]
                * outs[h]
                for h in every
            ],
        )
        square = jnp.sum(square, axis=1, keepdims=True)
        inner = jnp.sum(inner, axis=1, keepdims=True)
        placed = jnp.where(lane == n, square, 0.0) + jnp.where(lane == n + lanes, inner, 0.0)
        for h in every:
            low[state_rows(n, h, heads), :] = states[h]
            attended[rows, head(h)] = outs[h]
        sums[...] += placed
        return carried

    lax.fori_loop(0, blocks, step, 0, unroll=UNROLL)
    if not own:
        message[...] = jnp.transpose(sums[...])[: 2 * lanes, :]


def mixed(own, blocks, heads, lanes, parts, docs, *rest):
    if not own:
        pieces, rest = rest[:parts], rest[parts:]
        attended, q, g, gain, grad, inside, message, scale, slope, running, turn = rest
        total = pieces[0][...]
        for piece in pieces[1:]:
            total = total + piece[...]
        r = lax.rsqrt(total[:lanes] / QW + epsilon)
        s = r * r * r * (total[lanes:] / QW)
        turn[...] = jnp.zeros((HD, C), F32)
        turn[:lanes, :] = r
        turn[lanes : 2 * lanes, :] = s
        columns = jnp.transpose(turn[...])
        for n in range(blocks):
            rows = pl.ds(n * C, C)
            scale[rows, :] = jnp.broadcast_to(columns[:, n : n + 1], (C, HD))
            slope[rows, :] = jnp.broadcast_to(columns[:, lanes + n : lanes + n + 1], (C, HD))
    else:
        scale, slope, attended, q, g, gain, grad, inside, message, running = rest
    off = half_start(own, heads * HD)
    gains = gain[:, pl.ds(off, heads * HD)]
    running[...] = jnp.zeros((heads * HD, HD), F32)
    every = range(heads)

    def step(i, carried):
        n = blocks - 1 - i
        rows = block(n)
        linked = docs[n] == docs[jnp.maximum(n - 1, 0)]
        r = scale[rows, :]
        s = slope[rows, :]
        ds = []
        for h in every:
            weighted = g[rows, pl.ds(off + h * HD, HD)].astype(F32)
            weighted = weighted * gains[:, h * HD : (h + 1) * HD]
            ds.append((r * weighted - attended[rows, head(h)] * s).astype(BF16))
        sums = [dot(q[rows, pl.ds(off + h * HD, HD)], ds[h], TN) for h in every]
        befores = [running[head(h), :] for h in every]
        for h in every:
            grad[rows, head(h)] = ds[h]
            inside[state_rows(n, h, heads), :] = befores[h]
            total = befores[h] + sums[h]
            message[head(h), :] = total
            running[head(h), :] = jnp.where(linked, total, 0.0)
        return carried

    lax.fori_loop(0, blocks, step, 0, unroll=UNROLL)
    message[heads * HD :, :] = jnp.full((PAD, HD), -docs[0].astype(F32), F32)


def store_blocks(n, pairs, cols, sems):
    slot = lax.rem(n, 2)
    return [
        pltpu.make_async_copy(stage.at[slot], out.at[block(n), cols], sems.at[i, slot])
        for i, (stage, out) in enumerate(pairs)
    ]


def query_side(own, blocks, heads, after, k, v, q, attended, scale, gain, grad, low, scores, *rest):
    rest = rest[2:] if own else rest
    normed, query_grad, key_local, value_local, done, stage_n, stage_q, sems = rest
    off = half_start(own, heads * HD)
    cols = pl.ds(off, heads * HD)
    gains = gain[:, cols]
    pairs = ((stage_n, normed), (stage_q, query_grad))
    causal = causal_mask()
    every = range(heads)

    def step(n, carried):
        rows = block(n)
        slot = lax.rem(n, 2)

        @pl.when(n >= 2)
        def _():
            for copy in store_blocks(n - 2, pairs, cols, sems):
                copy.wait()

        r = scale[rows, :]
        ds = [grad[rows, head(h)] for h in every]
        raw = [dot(ds[h], v[rows, head(h)], NT) for h in every]
        gs = [jnp.where(causal, x, 0.0).astype(BF16) for x in raw]
        qg = [
            dot(ds[h], low[state_rows(n, h, heads), :], NT) + dot(gs[h], k[rows, head(h)], NN)
            for h in every
        ]
        kg = [dot(gs[h], q[rows, pl.ds(off + h * HD, HD)], TN) for h in every]
        vg = [dot(scores[score_rows(n, h, heads), :], ds[h], TN) for h in every]
        outs = [
            attended[rows, head(h)] * r * gains[:, h * HD : (h + 1) * HD] for h in every
        ]
        for h in every:
            stage_q[slot, :, head(h)] = qg[h].astype(BF16)
            stage_n[slot, :, head(h)] = outs[h].astype(BF16)
            key_local[rows, head(h)] = kg[h]
            value_local[rows, head(h)] = vg[h]
        for copy in store_blocks(n, pairs, cols, sems):
            copy.start()
        return carried

    lax.fori_loop(0, blocks, step, 0)
    for n in range(max(blocks - 2, 0), blocks):
        for copy in store_blocks(n, pairs, cols, sems):
            copy.wait()
    done[...] = jnp.zeros(done.shape, F32)


def key_side(own, blocks, heads, docs, inside, carry, k, v, key_local, value_local, *rest):
    rest = rest if own else rest[2:]
    key_grad, value_grad, stage_k, stage_v, sems = rest
    off = half_start(own, heads * HD)
    cols = pl.ds(off, heads * HD)
    pairs = ((stage_k, key_grad), (stage_v, value_grad))
    every = range(heads)

    def step(n, carried):
        rows = block(n)
        slot = lax.rem(n, 2)

        @pl.when(n >= 2)
        def _():
            for copy in store_blocks(n - 2, pairs, cols, sems):
                copy.wait()

        hit = carry[heads * HD : heads * HD + 1, :] == -docs[n].astype(F32)
        states = []
        for h in every:
            state = inside[state_rows(n, h, heads), :] + jnp.where(hit, carry[head(h), :], 0.0)
            states.append(state.astype(BF16))
        kg = [dot(v[rows, head(h)], states[h], NT) for h in every]
        vg = [dot(k[rows, head(h)], states[h], NN) for h in every]
        kg = [(kg[h] + key_local[rows, head(h)]).astype(BF16) for h in every]
        vg = [(vg[h] + value_local[rows, head(h)]).astype(BF16) for h in every]
        for h in every:
            stage_k[slot, :, head(h)] = kg[h]
            stage_v[slot, :, head(h)] = vg[h]
        for copy in store_blocks(n, pairs, cols, sems):
            copy.start()
        return carried

    lax.fori_loop(0, blocks, step, 0)
    for n in range(max(blocks - 2, 0), blocks):
        for copy in store_blocks(n, pairs, cols, sems):
            copy.wait()


def merge_kernel(reverse, outs, count, *refs):
    size = lax.axis_size("ctx")
    rank = lax.axis_index("ctx")
    if reverse:
        rank = size - 1 - rank

    def bit(b):
        return lax.rem(lax.div(rank, 1 << b), 2)

    ins, results = refs[:count], refs[count:]
    for pieces, result in zip(outs, results):
        at = 0
        latest = None
        for rows, terms in pieces:
            keys = []
            for source, start, flag in terms:
                last = ins[source].shape[0] - PAD
                key = ins[source][last : last + 1, :]
                keys.append(key if flag is None else jnp.where(flag(bit), key, NEVER))
            latest = functools.reduce(jnp.maximum, keys)
            value = None
            for (source, start, _), key in zip(terms, keys):
                part = jnp.where(key == latest, ins[source][start : start + rows, :], 0.0)
                value = part if value is None else value + part
            result[at : at + rows, :] = value
            at += rows
        result[at:, :] = jnp.broadcast_to(latest, (PAD, HD))


def merge(ins, outs, reverse, after=()):
    shapes = [pltpu.VMEM((sum(rows for rows, _ in pieces) + PAD, HD), F32) for pieces in outs]
    ins = list(ins) + list(after)
    return pl.pallas_call(
        functools.partial(merge_kernel, reverse, outs, len(ins)),
        name="merge",
        out_shape=shapes,
        in_specs=[VM] * len(ins),
        out_specs=[VM] * len(outs),
        compiler_params=params(),
        cost_estimate=cost(0, 1 << 18),
    )(*ins)


def swap(message, b):
    size = lax.axis_size("ctx")
    return lax.ppermute(message, "ctx", [(i, i ^ (1 << b)) for i in range(size)])


def scan(theirs, mine, reverse, first_work, second_work):
    rows = mine.shape[0] - PAD
    part = rows // 2
    top = lax.axis_size("ctx").bit_length() - 1
    lo, hi = top - 2, top - 1
    beside = swap(theirs, 0)
    halves = [[(part, [(0, start, None), (1, start, None)])] for start in (0, part)]
    total_a, total_b = merge([mine, beside], halves, reverse)
    before_a, before_b = [], []
    for b in range(1, lo):
        got_a, got_b = swap(total_a, b), swap(total_b, b)

        def is_high(bit, b=b):
            return bit(b) == 1

        ins = [total_a, total_b, got_a, got_b] + before_a + before_b
        earlier_a = [(4, 0, None)] if before_a else []
        earlier_b = [(5, 0, None)] if before_b else []
        total_a, total_b, pa, pb = merge(
            ins,
            [
                [(part, [(0, 0, None), (2, 0, None)])],
                [(part, [(1, 0, None), (3, 0, None)])],
                [(part, [(2, 0, is_high)] + earlier_a)],
                [(part, [(3, 0, is_high)] + earlier_b)],
            ],
            reverse,
        )
        before_a, before_b = [pa], [pb]
    first_a, first_b = swap(total_a, lo), swap(total_b, hi)
    first_done = first_work(total_a)
    next_a, next_b = merge(
        [total_a, first_a, total_b, first_b],
        [
            [(part, [(0, 0, None), (1, 0, None)])],
            [
                (
                    part,
                    [
                        (2, 0, lambda bit: bit(lo) * bit(hi) == 0),
                        (3, 0, lambda bit: bit(hi) == 1),
                    ],
                )
            ],
        ],
        reverse,
        first_done[-1:],
    )
    second_a, second_b = swap(next_a, hi), swap(next_b, lo)
    second_done = second_work(next_a, first_done)

    def carried(neighbour, flag):
        terms_a = [(0, 0, lambda bit: bit(lo) == 1), (1, 0, lambda bit: bit(hi) == 1)]
        terms_b = [(2, 0, lambda bit: bit(hi) == 1), (3, 0, lambda bit: bit(lo) + bit(hi) > 0)]
        if before_a:
            terms_a.append((6, 0, None))
            terms_b.append((7, 0, None))
        return [
            (part, terms_a + [(neighbour, 0, flag)]),
            (part, terms_b + [(neighbour, part, flag)]),
        ]

    carry_mine, carry_theirs = merge(
        [first_a, second_a, first_b, second_b, beside, mine] + before_a + before_b,
        [carried(4, lambda bit: bit(0) == 1), carried(5, lambda bit: bit(0) == 0)],
        reverse,
        second_done[-1:],
    )
    return carry_mine, swap(carry_theirs, 0), first_done[:-1], second_done[:-1]


def local(queries, keys, values, out_grad, gain, doc_ids):
    tokens, features = queries.shape
    heads = features // HD // 2
    cols = heads * HD
    blocks = tokens // C
    lanes = -(-blocks // 8) * 8
    pairs = blocks * heads
    tp = lax.axis_size("tp")
    gain = gain.reshape(1, features)
    rows = cols + PAD
    narrow, wide, square = C * HD * HD, C * C * HD, HD * HD
    dma = pltpu.SemaphoreType.DMA
    half_bf = pltpu.VMEM((tokens, cols), BF16)
    half_f32 = pltpu.VMEM((tokens, cols), F32)
    states_f32 = pltpu.VMEM((pairs * HD, HD), F32)
    message = pltpu.VMEM((rows, HD), F32)
    whole = pltpu.HBM((tokens, features), BF16)
    column = pltpu.VMEM((tokens, HD), F32)

    keys, values = [pltpu.with_memory_space_constraint(x, pltpu.HBM) for x in (keys, values)]
    queries, out_grad = [
        pltpu.with_memory_space_constraint(x, pltpu.VMEM) for x in (queries, out_grad)
    ]
    token = pltpu.VMEM((PAD, HD), F32)

    def states(own):
        return pl.pallas_call(
            functools.partial(key_value_states, own, blocks, heads),
            name=label("states", own),
            out_shape=[half_bf, half_bf, states_f32, message],
            in_specs=[SM, HB, HB],
            out_specs=[VM] * 4,
            scratch_shapes=[dma((2 * heads,))],
            compiler_params=params(),
            cost_estimate=cost(2 * pairs * narrow, 4 * tokens * cols),
        )(doc_ids, keys, values)

    def scoring(own, k, v, after):
        return pl.pallas_call(
            functools.partial(local_scores, own, blocks, heads),
            name=label("scoring", own),
            out_shape=[half_f32, pltpu.VMEM((pairs * C, C), BF16), token],
            in_specs=[VM] * 4,
            out_specs=[VM] * 3,
            compiler_params=params(),
            cost_estimate=cost(4 * pairs * wide, 4 * tokens * cols),
        )(after, k, v, queries)

    def attending(own, inside, carry, sv, sums):
        ins = [doc_ids, inside, carry, queries, sv, out_grad, gain] + ([] if own else [sums])
        last = [pltpu.VMEM((C, HD), F32)] if own else [pltpu.VMEM((2 * lanes, C), F32)]
        return pl.pallas_call(
            functools.partial(attend, own, blocks, heads, lanes),
            name=label("attend", own),
            out_shape=[half_f32, pltpu.VMEM((pairs * HD, HD), BF16)] + last,
            in_specs=[SM] + [VM] * (len(ins) - 1),
            out_specs=[VM] * 3,
            scratch_shapes=[] if own else [pltpu.VMEM((C, HD), F32)],
            input_output_aliases={4: 0},
            compiler_params=params(),
            cost_estimate=cost(2 * pairs * narrow, 1 << 20),
        )(*ins)

    def mixing(own, before, attended):
        ins = [doc_ids] + before + [attended, queries, out_grad, gain]
        outs = [half_bf, states_f32, message] + ([] if own else [column, column])
        scratch = [pltpu.VMEM((cols, HD), F32)]
        return pl.pallas_call(
            functools.partial(mixed, own, blocks, heads, lanes, tp),
            name=label("mixed", own),
            out_shape=outs,
            in_specs=[SM] + [VM] * (len(ins) - 1),
            out_specs=[VM] * len(outs),
            scratch_shapes=scratch if own else scratch + [pltpu.VMEM((HD, C), F32)],
            compiler_params=params(),
            cost_estimate=cost(2 * pairs * narrow, 1 << 20),
        )(*ins)

    def query_grads(own, k, v, attended, scale, grad, low, scores, so_far, after):
        ins = [after, k, v, queries, attended, scale, gain, grad, low, scores] + list(so_far)
        stage = pltpu.VMEM((2, C, cols), BF16)
        return pl.pallas_call(
            functools.partial(query_side, own, blocks, heads),
            name=label("query_side", own),
            out_shape=[whole, whole, half_f32, half_f32, token],
            in_specs=[VM] * 10 + [HB] * len(so_far),
            out_specs=[HB, HB, VM, VM, VM],
            scratch_shapes=[stage, stage, dma((2, 2))],
            input_output_aliases={10: 0, 11: 1} if own else {},
            compiler_params=params(),
            cost_estimate=cost(8 * pairs * wide, 4 * tokens * cols),
        )(*ins)

    def key_grads(own, inside, carry, k, v, key_local, value_local, so_far):
        ins = [doc_ids, inside, carry, k, v, key_local, value_local] + list(so_far)
        stage = pltpu.VMEM((2, C, cols), BF16)
        return pl.pallas_call(
            functools.partial(key_side, own, blocks, heads),
            name=label("key_side", own),
            out_shape=[whole, whole],
            in_specs=[SM] + [VM] * 6 + [HB] * len(so_far),
            out_specs=[HB, HB],
            scratch_shapes=[stage, stage, dma((2, 2))],
            input_output_aliases={} if own else {7: 0, 8: 1},
            compiler_params=params(),
            cost_estimate=cost(4 * pairs * narrow, 4 * tokens * cols),
        )(*ins)

    k1, v1, inside1, theirs = states(False)
    k0, v0, inside0, mine = states(True)
    carry0, carry1, (local1, scores1), (local0, scores0) = scan(
        theirs,
        mine,
        False,
        lambda after: scoring(False, k1, v1, after),
        lambda after, _: scoring(True, k0, v0, after),
    )
    att0, low0, sums = attending(True, inside0, carry0, local0, None)
    att1, low1, sums = attending(False, inside1, carry1, local1, sums)
    parts = [sums] + [
        lax.ppermute(sums, "tp", [(i, (i + s) % tp) for i in range(tp)]) for s in range(1, tp)
    ]
    grad1, after1, theirs, scale, slope = mixing(False, parts, att1)
    grad0, after0, mine = mixing(True, [scale, slope], att0)
    carry0, carry1, (_, _, kl1, vl1), (normed, query_grad, kl0, vl0) = scan(
        theirs,
        mine,
        True,
        lambda after: query_grads(False, k1, v1, att1, scale, grad1, low1, scores1, (), after),
        lambda after, done: query_grads(
            True, k0, v0, att0, scale, grad0, low0, scores0, done[:2], after
        ),
    )
    key_grad, value_grad = key_grads(True, after0, carry0, k0, v0, kl0, vl0, ())
    key_grad, value_grad = key_grads(
        False, after1, carry1, k1, v1, kl1, vl1, (key_grad, value_grad)
    )
    return normed, query_grad, key_grad, value_grad


def solution(mesh):
    return jax.shard_map(
        local,
        mesh=mesh,
        in_specs=(
            P("ctx", "tp"),
            P("ctx", "tp"),
            P("ctx", "tp"),
            P("ctx", "tp"),
            P("tp"),
            P("ctx"),
        ),
        out_specs=(P("ctx", "tp"), P("ctx", "tp"), P("ctx", "tp"), P("ctx", "tp")),
        check_vma=False,
    )
```

```python
import functools

import jax
import jax.numpy as jnp
from jax import lax
from jax.experimental import pallas as pl
from jax.experimental.pallas import tpu as pltpu
from jax.sharding import PartitionSpec as P

HD = 128
C = 256
QW = 4096
PAD = 8
NEVER = -1.0e9
MIB = 1 << 20
U_SCORE = 6
U_ATT = 6
U_MIX = 6
U_Q = 6
U_K = 6
T_ATT = 128
T_MIX = 128

epsilon = 1e-06

F32 = jnp.float32
BF16 = jnp.bfloat16
VM = pl.BlockSpec(memory_space=pltpu.VMEM)
HB = pl.BlockSpec(memory_space=pltpu.HBM)


def dot(a, b, dims):
    return lax.dot_general(a, b, (dims, ((), ())), preferred_element_type=F32)


NN = ((1,), (0,))
NT = ((1,), (1,))
TN = ((0,), (0,))


def params(mib=12):
    return pltpu.CompilerParams(vmem_limit_bytes=mib * MIB)


def cost(flops, nbytes):
    return pl.CostEstimate(flops=int(flops), bytes_accessed=int(nbytes), transcendentals=0)


def half_start(own, cols):
    core = lax.rem(lax.axis_index("ctx"), 2)
    half = core if own else 1 - core
    return pl.multiple_of(half * cols, 128)


def label(name, own):
    return name + ("_own" if own else "_other")


def head(h):
    return pl.ds(h * HD, HD)


def block(n):
    return pl.ds(pl.multiple_of(n * C, C), C)


def state_rows(n, h, heads):
    return pl.ds(pl.multiple_of((n * heads + h) * HD, HD), HD)


def key_value_states(own, blocks, heads, docs_hbm, k_hbm, v_hbm, *rest):
    if own:
        k, v, inside, message, docs, sems = rest
    else:
        k, v, inside, message, table, docs, sems = rest
    off = half_start(own, heads * HD)
    docs_copy = pltpu.make_async_copy(docs_hbm, docs, sems.at[2 * heads])
    width = 2 * HD if heads % 2 == 0 else HD
    copies = []
    for i in range(heads * HD // width):
        src, dst = pl.ds(off + i * width, width), pl.ds(i * width, width)
        pair = (
            pltpu.make_async_copy(k_hbm.at[:, src], k.at[:, dst], sems.at[2 * i]),
            pltpu.make_async_copy(v_hbm.at[:, src], v.at[:, dst], sems.at[2 * i + 1]),
        )
        for copy in pair:
            copy.start()
        copies.append(pair)
    docs_copy.start()
    docs_copy.wait()
    for h in range(heads):
        if h * HD % width == 0:
            for copy in copies[h * HD // width]:
                copy.wait()
        per_block = [pl.ds(n * C, C) for n in range(blocks)]
        sums = [dot(k[rows, head(h)], v[rows, head(h)], TN) for rows in per_block]
        running = jnp.zeros((HD, HD), F32)
        for n in range(blocks):
            inside[state_rows(n, h, heads), :] = running
            total = running + sums[n]
            if n + 1 < blocks:
                running = jnp.where(docs[n] == docs[n + 1], total, 0.0)
            else:
                message[head(h), :] = total
    message[heads * HD :, :] = jnp.full((PAD, HD), docs[blocks - 1].astype(F32), F32)
    if not own:
        table[...] = jnp.zeros(table.shape, F32)
        for n in range(blocks):
            table[n : n + 1, :] = jnp.full((1, HD), docs[n].astype(F32), F32)


def causal_mask():
    return lax.broadcasted_iota(jnp.int32, (C, C), 0) >= lax.broadcasted_iota(jnp.int32, (C, C), 1)


def score_rows(n, h, heads):
    return pl.ds(pl.multiple_of((n * heads + h) * C, C), C)


def local_scores(
    own, blocks, heads, after, k, v, q_hbm, g_hbm, q, g, local, scores, done, q_sems, g_sem
):
    cols = pl.ds(half_start(own, heads * HD), heads * HD)

    def q_copy(n):
        return pltpu.make_async_copy(q_hbm.at[block(n), cols], q.at[block(n), :], q_sems.at[n])

    for n in range(blocks):
        q_copy(n).start()
    g_copy = pltpu.make_async_copy(g_hbm.at[:, cols], g, g_sem)
    g_copy.start()
    causal = causal_mask()
    every = range(heads)

    def step(n, carry):
        q_copy(n).wait()
        rows = block(n)
        raw = [dot(q[rows, head(h)], k[rows, head(h)], NT) for h in every]
        low = [jnp.where(causal, s, 0.0).astype(BF16) for s in raw]
        outs = [dot(low[h], v[rows, head(h)], NN) for h in every]
        for h in every:
            scores[score_rows(n, h, heads), :] = low[h]
            local[rows, head(h)] = outs[h]
        return carry

    lax.fori_loop(0, blocks, step, 0, unroll=U_SCORE)
    g_copy.wait()
    done[...] = jnp.zeros(done.shape, F32)


def attend(own, blocks, heads, lanes, docs, inside, carry, q, local, g, gain, *rest):
    if own:
        attended, low, sums = rest
        sums[...] = jnp.zeros((C, HD), F32)
    else:
        sums_in, attended, low, message, sums = rest
        sums[...] = sums_in[...]
    off = half_start(own, heads * HD)
    gains = gain[:, pl.ds(off, heads * HD)]
    lane = lax.broadcasted_iota(jnp.int32, (T_ATT, HD), 1)
    every = range(heads)

    def step(n, carried):
        hit = carry[heads * HD : heads * HD + 1, :] == docs[pl.ds(n, 1), :]
        states = []
        for h in every:
            state = inside[state_rows(n, h, heads), :] + jnp.where(hit, carry[head(h), :], 0.0)
            states.append(state.astype(BF16))
            low[state_rows(n, h, heads), :] = states[h]
        for t in range(0, C, T_ATT):
            rows = pl.ds(pl.multiple_of(n * C + t, T_ATT), T_ATT)
            square = jnp.zeros((T_ATT, HD), F32)
            inner = jnp.zeros((T_ATT, HD), F32)
            for h in every:
                out = local[rows, head(h)] + dot(q[rows, head(h)], states[h], NN)
                attended[rows, head(h)] = out
                square += out * out
                weighted = g[rows, head(h)].astype(F32) * gains[:, h * HD : (h + 1) * HD]
                inner += weighted * out
            square = jnp.sum(square, axis=1, keepdims=True)
            inner = jnp.sum(inner, axis=1, keepdims=True)
            sums[t : t + T_ATT, :] += jnp.where(lane == n, square, 0.0) + jnp.where(
                lane == n + lanes, inner, 0.0
            )
        return carried

    lax.fori_loop(0, blocks, step, 0, unroll=U_ATT)
    if not own:
        message[...] = jnp.transpose(sums[...])[: 2 * lanes, :]


def mixed(own, blocks, heads, lanes, parts, docs, *rest):
    if not own:
        pieces, rest = rest[:parts], rest[parts:]
        attended, q, g, gain, grad, inside, message, scale, slope, running, turn = rest
        total = pieces[0][...]
        for piece in pieces[1:]:
            total = total + piece[...]
        r = lax.rsqrt(total[:lanes] / QW + epsilon)
        s = r * r * r * (total[lanes:] / QW)
        turn[...] = jnp.zeros((HD, C), F32)
        turn[:lanes, :] = r
        turn[lanes : 2 * lanes, :] = s
        columns = jnp.transpose(turn[...])
        for n in range(blocks):
            rows = pl.ds(n * C, C)
            scale[rows, :] = jnp.broadcast_to(columns[:, n : n + 1], (C, HD))
            slope[rows, :] = jnp.broadcast_to(columns[:, lanes + n : lanes + n + 1], (C, HD))
    else:
        scale, slope, attended, q, g, gain, grad, inside, message, running = rest
    off = half_start(own, heads * HD)
    gains = gain[:, pl.ds(off, heads * HD)]
    running[...] = jnp.zeros((heads * HD, HD), F32)
    every = range(heads)

    def step(i, carried):
        n = blocks - 1 - i
        rows = block(n)
        linked = docs[pl.ds(n, 1), :] == docs[pl.ds(jnp.maximum(n - 1, 0), 1), :]
        for t in range(0, C, T_MIX):
            part = pl.ds(pl.multiple_of(n * C + t, T_MIX), T_MIX)
            r = scale[part, :]
            s = slope[part, :]
            for h in every:
                weighted = g[part, head(h)].astype(F32) * gains[:, h * HD : (h + 1) * HD]
                d = r * weighted - attended[part, head(h)] * s
                grad[part, head(h)] = d.astype(BF16)
        sums = [dot(q[rows, head(h)], grad[rows, head(h)], TN) for h in every]
        befores = [running[head(h), :] for h in every]
        for h in every:
            inside[state_rows(n, h, heads), :] = befores[h]
            total = befores[h] + sums[h]
            message[head(h), :] = total
            running[head(h), :] = jnp.where(linked, total, 0.0)
        return carried

    lax.fori_loop(0, blocks, step, 0, unroll=U_MIX)
    message[heads * HD :, :] = jnp.broadcast_to(-docs[0:1, :], (PAD, HD))


def store_blocks(n, slot, pairs, cols, sems):
    return [
        pltpu.make_async_copy(stage.at[slot], out.at[block(n), cols], sems.at[i, slot])
        for i, (stage, out) in enumerate(pairs)
    ]


def query_side(own, blocks, heads, after, k, v, q, attended, scale, gain, grad, low, scores, *rest):
    rest = rest[2:] if own else rest
    normed, query_grad, key_local, value_local, done, stage_n, stage_q, sems = rest
    off = half_start(own, heads * HD)
    cols = pl.ds(off, heads * HD)
    gains = gain[:, cols]
    pairs = ((stage_n, normed), (stage_q, query_grad))
    causal = causal_mask()
    every = range(heads)

    def step(n, carried):
        rows = block(n)
        r = scale[rows, :]
        ds = [grad[rows, head(h)] for h in every]
        raw = [dot(ds[h], v[rows, head(h)], NT) for h in every]
        gs = [jnp.where(causal, x, 0.0).astype(BF16) for x in raw]
        qg = [
            dot(ds[h], low[state_rows(n, h, heads), :], NT) + dot(gs[h], k[rows, head(h)], NN)
            for h in every
        ]
        kg = [dot(gs[h], q[rows, head(h)], TN) for h in every]
        vg = [dot(scores[score_rows(n, h, heads), :], ds[h], TN) for h in every]
        outs = [
            attended[rows, head(h)] * r * gains[:, h * HD : (h + 1) * HD] for h in every
        ]
        for h in every:
            stage_q[n, :, head(h)] = qg[h].astype(BF16)
            stage_n[n, :, head(h)] = outs[h].astype(BF16)
            key_local[rows, head(h)] = kg[h]
            value_local[rows, head(h)] = vg[h]
        for copy in store_blocks(n, n, pairs, cols, sems):
            copy.start()
        return carried

    lax.fori_loop(0, blocks, step, 0, unroll=U_Q)
    for n in range(blocks):
        for copy in store_blocks(n, n, pairs, cols, sems):
            copy.wait()
    done[...] = jnp.zeros(done.shape, F32)


def key_side(own, blocks, heads, docs, inside, carry, k, v, key_local, value_local, *rest):
    rest = rest if own else rest[2:]
    key_grad, value_grad, stage_k, stage_v, sems = rest
    off = half_start(own, heads * HD)
    cols = pl.ds(off, heads * HD)
    pairs = ((stage_k, key_grad), (stage_v, value_grad))
    every = range(heads)

    def step(n, carried):
        rows = block(n)
        hit = carry[heads * HD : heads * HD + 1, :] == -docs[pl.ds(n, 1), :]
        states = []
        for h in every:
            state = inside[state_rows(n, h, heads), :] + jnp.where(hit, carry[head(h), :], 0.0)
            states.append(state.astype(BF16))
        kg = [dot(v[rows, head(h)], states[h], NT) for h in every]
        vg = [dot(k[rows, head(h)], states[h], NN) for h in every]
        kg = [(kg[h] + key_local[rows, head(h)]).astype(BF16) for h in every]
        vg = [(vg[h] + value_local[rows, head(h)]).astype(BF16) for h in every]
        for h in every:
            stage_k[n, :, head(h)] = kg[h]
            stage_v[n, :, head(h)] = vg[h]
        for copy in store_blocks(n, n, pairs, cols, sems):
            copy.start()
        return carried

    lax.fori_loop(0, blocks, step, 0, unroll=U_K)
    for n in range(blocks):
        for copy in store_blocks(n, n, pairs, cols, sems):
            copy.wait()


def merge_kernel(reverse, outs, count, *refs):
    size = lax.axis_size("ctx")
    rank = lax.axis_index("ctx")
    if reverse:
        rank = size - 1 - rank

    def bit(b):
        return lax.rem(lax.div(rank, 1 << b), 2)

    ins, results = refs[:count], refs[count:]
    for pieces, result in zip(outs, results):
        at = 0
        latest = None
        for rows, terms in pieces:
            keys = []
            for source, start, flag in terms:
                last = ins[source].shape[0] - PAD
                key = ins[source][last : last + 1, :]
                keys.append(key if flag is None else jnp.where(flag(bit), key, NEVER))
            latest = functools.reduce(jnp.maximum, keys)
            value = None
            for (source, start, _), key in zip(terms, keys):
                part = jnp.where(key == latest, ins[source][start : start + rows, :], 0.0)
                value = part if value is None else value + part
            result[at : at + rows, :] = value
            at += rows
        result[at:, :] = jnp.broadcast_to(latest, (PAD, HD))


def merge(ins, outs, reverse, after=()):
    shapes = [pltpu.VMEM((sum(rows for rows, _ in pieces) + PAD, HD), F32) for pieces in outs]
    ins = list(ins) + list(after)
    return pl.pallas_call(
        functools.partial(merge_kernel, reverse, outs, len(ins)),
        name="merge",
        out_shape=shapes,
        in_specs=[VM] * len(ins),
        out_specs=[VM] * len(outs),
        compiler_params=params(),
        cost_estimate=cost(0, 1 << 18),
    )(*ins)


def swap(message, b):
    size = lax.axis_size("ctx")
    return lax.ppermute(message, "ctx", [(i, i ^ (1 << b)) for i in range(size)])


def scan(theirs, mine, reverse, first_work, second_work):
    rows = mine.shape[0] - PAD
    part = rows // 2
    top = lax.axis_size("ctx").bit_length() - 1
    lo, hi = top - 2, top - 1
    beside = swap(theirs, 0)
    halves = [[(part, [(0, start, None), (1, start, None)])] for start in (0, part)]
    total_a, total_b = merge([mine, beside], halves, reverse)
    before_a, before_b = [], []
    for b in range(1, lo):
        got_a, got_b = swap(total_a, b), swap(total_b, b)

        def is_high(bit, b=b):
            return bit(b) == 1

        ins = [total_a, total_b, got_a, got_b] + before_a + before_b
        earlier_a = [(4, 0, None)] if before_a else []
        earlier_b = [(5, 0, None)] if before_b else []
        total_a, total_b, pa, pb = merge(
            ins,
            [
                [(part, [(0, 0, None), (2, 0, None)])],
                [(part, [(1, 0, None), (3, 0, None)])],
                [(part, [(2, 0, is_high)] + earlier_a)],
                [(part, [(3, 0, is_high)] + earlier_b)],
            ],
            reverse,
        )
        before_a, before_b = [pa], [pb]
    first_a, first_b = swap(total_a, lo), swap(total_b, hi)
    first_done = first_work(total_a)
    next_a, next_b = merge(
        [total_a, first_a, total_b, first_b],
        [
            [(part, [(0, 0, None), (1, 0, None)])],
            [
                (
                    part,
                    [
                        (2, 0, lambda bit: bit(lo) * bit(hi) == 0),
                        (3, 0, lambda bit: bit(hi) == 1),
                    ],
                )
            ],
        ],
        reverse,
        first_done[-1:],
    )
    second_a, second_b = swap(next_a, hi), swap(next_b, lo)
    second_done = second_work(next_a, first_done)

    def carried(neighbour, flag):
        terms_a = [(0, 0, lambda bit: bit(lo) == 1), (1, 0, lambda bit: bit(hi) == 1)]
        terms_b = [(2, 0, lambda bit: bit(hi) == 1), (3, 0, lambda bit: bit(lo) + bit(hi) > 0)]
        if before_a:
            terms_a.append((6, 0, None))
            terms_b.append((7, 0, None))
        return [
            (part, terms_a + [(neighbour, 0, flag)]),
            (part, terms_b + [(neighbour, part, flag)]),
        ]

    carry_mine, carry_theirs = merge(
        [first_a, second_a, first_b, second_b, beside, mine] + before_a + before_b,
        [carried(4, lambda bit: bit(0) == 1), carried(5, lambda bit: bit(0) == 0)],
        reverse,
        second_done[-1:],
    )
    return carry_mine, swap(carry_theirs, 0), first_done[:-1], second_done[:-1]


def local(queries, keys, values, out_grad, gain, doc_ids):
    tokens, features = queries.shape
    heads = features // HD // 2
    cols = heads * HD
    blocks = tokens // C
    lanes = -(-blocks // 8) * 8
    pairs = blocks * heads
    tp = lax.axis_size("tp")
    gain = gain.reshape(1, features)
    rows = cols + PAD
    narrow, wide, square = C * HD * HD, C * C * HD, HD * HD
    dma = pltpu.SemaphoreType.DMA
    half_bf = pltpu.VMEM((tokens, cols), BF16)
    half_f32 = pltpu.VMEM((tokens, cols), F32)
    states_f32 = pltpu.VMEM((pairs * HD, HD), F32)
    message = pltpu.VMEM((rows, HD), F32)
    whole = pltpu.HBM((tokens, features), BF16)
    column = pltpu.VMEM((tokens, HD), F32)

    keys, values, queries, out_grad, docs_hbm = [
        pltpu.with_memory_space_constraint(x, pltpu.HBM)
        for x in (keys, values, queries, out_grad, doc_ids)
    ]
    token = pltpu.VMEM((PAD, HD), F32)

    def states(own):
        outs = [half_bf, half_bf, states_f32, message]
        outs += [] if own else [pltpu.VMEM((lanes, HD), F32)]
        return pl.pallas_call(
            functools.partial(key_value_states, own, blocks, heads),
            name=label("states", own),
            out_shape=outs,
            in_specs=[HB, HB, HB],
            out_specs=[VM] * len(outs),
            scratch_shapes=[pltpu.SMEM((blocks,), jnp.int32), dma((2 * heads + 1,))],
            compiler_params=params(),
            cost_estimate=cost(2 * pairs * narrow, 4 * tokens * cols),
        )(docs_hbm, keys, values)

    def scoring(own, k, v, after):
        return pl.pallas_call(
            functools.partial(local_scores, own, blocks, heads),
            name=label("scoring", own),
            out_shape=[half_bf, half_bf, half_f32, pltpu.VMEM((pairs * C, C), BF16), token],
            in_specs=[VM] * 3 + [HB] * 2,
            out_specs=[VM] * 5,
            scratch_shapes=[dma((blocks,)), dma],
            compiler_params=params(),
            cost_estimate=cost(4 * pairs * wide, 4 * tokens * cols),
        )(after, k, v, queries, out_grad)

    def attending(own, inside, carry, q, sv, g, sums):
        ins = [docs, inside, carry, q, sv, g, gain] + ([] if own else [sums])
        last = [pltpu.VMEM((C, HD), F32)] if own else [pltpu.VMEM((2 * lanes, C), F32)]
        return pl.pallas_call(
            functools.partial(attend, own, blocks, heads, lanes),
            name=label("attend", own),
            out_shape=[half_f32, pltpu.VMEM((pairs * HD, HD), BF16)] + last,
            in_specs=[VM] * len(ins),
            out_specs=[VM] * 3,
            scratch_shapes=[] if own else [pltpu.VMEM((C, HD), F32)],
            compiler_params=params(),
            cost_estimate=cost(2 * pairs * narrow, 1 << 20),
        )(*ins)

    def mixing(own, before, attended, q, g):
        ins = [docs] + before + [attended, q, g, gain]
        outs = [half_bf, states_f32, message] + ([] if own else [column, column])
        scratch = [pltpu.VMEM((cols, HD), F32)]
        return pl.pallas_call(
            functools.partial(mixed, own, blocks, heads, lanes, tp),
            name=label("mixed", own),
            out_shape=outs,
            in_specs=[VM] * len(ins),
            out_specs=[VM] * len(outs),
            scratch_shapes=scratch if own else scratch + [pltpu.VMEM((HD, C), F32)],
            compiler_params=params(),
            cost_estimate=cost(2 * pairs * narrow, 1 << 20),
        )(*ins)

    def query_grads(own, k, v, q, attended, scale, grad, low, scores, so_far, after):
        ins = [after, k, v, q, attended, scale, gain, grad, low, scores] + list(so_far)
        stage = pltpu.VMEM((blocks, C, cols), BF16)
        return pl.pallas_call(
            functools.partial(query_side, own, blocks, heads),
            name=label("query_side", own),
            out_shape=[whole, whole, half_f32, half_f32, token],
            in_specs=[VM] * 10 + [HB] * len(so_far),
            out_specs=[HB, HB, VM, VM, VM],
            scratch_shapes=[stage, stage, dma((2, blocks))],
            input_output_aliases={10: 0, 11: 1} if own else {},
            compiler_params=params(),
            cost_estimate=cost(8 * pairs * wide, 4 * tokens * cols),
        )(*ins)

    def key_grads(own, inside, carry, k, v, key_local, value_local, so_far):
        ins = [docs, inside, carry, k, v, key_local, value_local] + list(so_far)
        stage = pltpu.VMEM((blocks, C, cols), BF16)
        return pl.pallas_call(
            functools.partial(key_side, own, blocks, heads),
            name=label("key_side", own),
            out_shape=[whole, whole],
            in_specs=[VM] * 7 + [HB] * len(so_far),
            out_specs=[HB, HB],
            scratch_shapes=[stage, stage, dma((2, blocks))],
            input_output_aliases={} if own else {7: 0, 8: 1},
            compiler_params=params(),
            cost_estimate=cost(4 * pairs * narrow, 4 * tokens * cols),
        )(*ins)

    k1, v1, inside1, theirs, docs = states(False)
    k0, v0, inside0, mine = states(True)
    carry0, carry1, (q1, g1, local1, scores1), (q0, g0, local0, scores0) = scan(
        theirs,
        mine,
        False,
        lambda after: scoring(False, k1, v1, after),
        lambda after, _: scoring(True, k0, v0, after),
    )
    att0, low0, sums = attending(True, inside0, carry0, q0, local0, g0, None)
    att1, low1, sums = attending(False, inside1, carry1, q1, local1, g1, sums)
    parts = [sums] + [
        lax.ppermute(sums, "tp", [(i, (i + s) % tp) for i in range(tp)]) for s in range(1, tp)
    ]
    grad1, after1, theirs, scale, slope = mixing(False, parts, att1, q1, g1)
    grad0, after0, mine = mixing(True, [scale, slope], att0, q0, g0)
    carry0, carry1, (_, _, kl1, vl1), (normed, query_grad, kl0, vl0) = scan(
        theirs,
        mine,
        True,
        lambda after: query_grads(False, k1, v1, q1, att1, scale, grad1, low1, scores1, (), after),
        lambda after, done: query_grads(
            True, k0, v0, q0, att0, scale, grad0, low0, scores0, done[:2], after
        ),
    )
    key_grad, value_grad = key_grads(True, after0, carry0, k0, v0, kl0, vl0, ())
    key_grad, value_grad = key_grads(
        False, after1, carry1, k1, v1, kl1, vl1, (key_grad, value_grad)
    )
    return normed, query_grad, key_grad, value_grad


def solution(mesh):
    return jax.shard_map(
        local,
        mesh=mesh,
        in_specs=(
            P("ctx", "tp"),
            P("ctx", "tp"),
            P("ctx", "tp"),
            P("ctx", "tp"),
            P("tp"),
            P("ctx"),
        ),
        out_specs=(P("ctx", "tp"), P("ctx", "tp"), P("ctx", "tp"), P("ctx", "tp")),
        check_vma=False,
    )
```

```python
import functools

import jax
import jax.numpy as jnp
from jax import lax
from jax.experimental import pallas as pl
from jax.experimental.pallas import tpu as pltpu
from jax.sharding import PartitionSpec as P

HD = 128
C = 256
QW = 4096
PAD = 8
NEVER = -1.0e9
MIB = 1 << 20
U_SCORE = 6
U_ATT = 6
U_Q = 6
U_K = 6
T_ATT = 128
T_MIX = 128

epsilon = 1e-06

F32 = jnp.float32
BF16 = jnp.bfloat16
VM = pl.BlockSpec(memory_space=pltpu.VMEM)
HB = pl.BlockSpec(memory_space=pltpu.HBM)


def dot(a, b, dims):
    return lax.dot_general(a, b, (dims, ((), ())), preferred_element_type=F32)


NN = ((1,), (0,))
NT = ((1,), (1,))
TN = ((0,), (0,))


def params(mib=12):
    return pltpu.CompilerParams(vmem_limit_bytes=mib * MIB)


def cost(flops, nbytes):
    return pl.CostEstimate(flops=int(flops), bytes_accessed=int(nbytes), transcendentals=0)


def half_start(own, cols):
    core = lax.rem(lax.axis_index("ctx"), 2)
    half = core if own else 1 - core
    return pl.multiple_of(half * cols, 128)


def label(name, own):
    return name + ("_own" if own else "_other")


def head(h):
    return pl.ds(h * HD, HD)


def block(n):
    return pl.ds(pl.multiple_of(n * C, C), C)


def state_rows(n, h, heads):
    start = (n * heads + h) * HD
    return pl.ds(start if isinstance(start, int) else pl.multiple_of(start, HD), HD)


def key_value_states(own, blocks, heads, *refs):
    if own:
        k, docs_hbm, v_hbm, v, inside, message, docs, sems = refs
    else:
        docs_hbm, k_hbm, v_hbm, k, v, inside, message, table, k_own, docs, sems = refs
    off = half_start(own, heads * HD)
    docs_copy = pltpu.make_async_copy(docs_hbm, docs, sems.at[2 * heads])
    width = 2 * HD if heads % 2 == 0 else HD
    groups = heads * HD // width
    copies = []
    for i in range(groups):
        src, dst = pl.ds(off + i * width, width), pl.ds(i * width, width)
        copies.append([pltpu.make_async_copy(v_hbm.at[:, src], v.at[:, dst], sems.at[2 * i])])
        if not own:
            copies[i].append(
                pltpu.make_async_copy(k_hbm.at[:, src], k.at[:, dst], sems.at[2 * i + 1])
            )
        for copy in copies[i]:
            copy.start()
    docs_copy.start()
    if not own:
        ahead = pltpu.make_async_copy(
            k_hbm.at[:, pl.ds(half_start(True, heads * HD), heads * HD)],
            k_own,
            sems.at[2 * heads + 1],
        )
        ahead.start()
    docs_copy.wait()
    for h in range(heads):
        if h * HD % width == 0:
            for copy in copies[h * HD // width]:
                copy.wait()
        per_block = [pl.ds(n * C, C) for n in range(blocks)]
        sums = [dot(k[rows, head(h)], v[rows, head(h)], TN) for rows in per_block]
        running = jnp.zeros((HD, HD), F32)
        for n in range(blocks):
            inside[state_rows(n, h, heads), :] = running
            total = running + sums[n]
            if n + 1 < blocks:
                running = jnp.where(docs[n] == docs[n + 1], total, 0.0)
            else:
                message[head(h), :] = total
    message[heads * HD :, :] = jnp.full((PAD, HD), docs[blocks - 1].astype(F32), F32)
    if not own:
        table[...] = jnp.zeros(table.shape, F32)
        for n in range(blocks):
            table[n : n + 1, :] = jnp.full((1, HD), docs[n].astype(F32), F32)
        ahead.wait()


def causal_mask():
    return lax.broadcasted_iota(jnp.int32, (C, C), 0) >= lax.broadcasted_iota(jnp.int32, (C, C), 1)


def score_rows(n, h, heads):
    return pl.ds(pl.multiple_of((n * heads + h) * C, C), C)


def local_scores(
    own, blocks, heads, after, k, v, q_hbm, g_hbm, q, g, local, scores, done, q_sems, g_sem
):
    cols = pl.ds(half_start(own, heads * HD), heads * HD)

    def q_copy(n):
        return pltpu.make_async_copy(q_hbm.at[block(n), cols], q.at[block(n), :], q_sems.at[n])

    for n in range(blocks):
        q_copy(n).start()
    g_copy = pltpu.make_async_copy(g_hbm.at[:, cols], g, g_sem)
    g_copy.start()
    causal = causal_mask()
    every = range(heads)

    def step(n, carry):
        q_copy(n).wait()
        rows = block(n)
        raw = [dot(q[rows, head(h)], k[rows, head(h)], NT) for h in every]
        low = [jnp.where(causal, s, 0.0).astype(BF16) for s in raw]
        outs = [dot(low[h], v[rows, head(h)], NN) for h in every]
        for h in every:
            scores[score_rows(n, h, heads), :] = low[h]
            local[rows, head(h)] = outs[h]
        return carry

    lax.fori_loop(0, blocks, step, 0, unroll=U_SCORE)
    g_copy.wait()
    done[...] = jnp.zeros(done.shape, F32)


def attend(own, blocks, heads, lanes, docs, inside, carry, q, local, g, gain, *rest):
    if own:
        attended, low, sums = rest
        sums[...] = jnp.zeros((C, HD), F32)
    else:
        sums_in, attended, low, message, sums = rest
        sums[...] = sums_in[...]
    off = half_start(own, heads * HD)
    gains = gain[:, pl.ds(off, heads * HD)]
    lane = lax.broadcasted_iota(jnp.int32, (T_ATT, HD), 1)
    every = range(heads)

    def step(n, carried):
        hit = carry[heads * HD : heads * HD + 1, :] == docs[pl.ds(n, 1), :]
        states = []
        for h in every:
            state = inside[state_rows(n, h, heads), :] + jnp.where(hit, carry[head(h), :], 0.0)
            states.append(state.astype(BF16))
            low[state_rows(n, h, heads), :] = states[h]
        for t in range(0, C, T_ATT):
            rows = pl.ds(pl.multiple_of(n * C + t, T_ATT), T_ATT)
            square = jnp.zeros((T_ATT, HD), F32)
            inner = jnp.zeros((T_ATT, HD), F32)
            for h in every:
                out = local[rows, head(h)] + dot(q[rows, head(h)], states[h], NN)
                attended[rows, head(h)] = out
                square += out * out
                weighted = g[rows, head(h)].astype(F32) * gains[:, h * HD : (h + 1) * HD]
                inner += weighted * out
            square = jnp.sum(square, axis=1, keepdims=True)
            inner = jnp.sum(inner, axis=1, keepdims=True)
            sums[t : t + T_ATT, :] += jnp.where(lane == n, square, 0.0) + jnp.where(
                lane == n + lanes, inner, 0.0
            )
        return carried

    lax.fori_loop(0, blocks, step, 0, unroll=U_ATT)
    if not own:
        message[...] = jnp.transpose(sums[...])[: 2 * lanes, :]


def mixed(own, blocks, heads, lanes, parts, docs, *rest):
    if not own:
        pieces, rest = rest[:parts], rest[parts:]
        attended, q, g, gain, grad, inside, message, scale, slope, turn = rest
        total = pieces[0][...]
        for piece in pieces[1:]:
            total = total + piece[...]
        r = lax.rsqrt(total[:lanes] / QW + epsilon)
        s = r * r * r * (total[lanes:] / QW)
        turn[...] = jnp.zeros((HD, C), F32)
        turn[:lanes, :] = r
        turn[lanes : 2 * lanes, :] = s
        columns = jnp.transpose(turn[...])
        for n in range(blocks):
            rows = pl.ds(n * C, C)
            scale[rows, :] = jnp.broadcast_to(columns[:, n : n + 1], (C, HD))
            slope[rows, :] = jnp.broadcast_to(columns[:, lanes + n : lanes + n + 1], (C, HD))
    else:
        scale, slope, attended, q, g, gain, grad, inside, message = rest
    off = half_start(own, heads * HD)
    gains = gain[:, pl.ds(off, heads * HD)]
    every = range(heads)
    for h in every:
        inside[state_rows(blocks - 1, h, heads), :] = jnp.zeros((HD, HD), F32)
    for n in reversed(range(blocks)):
        rows = pl.ds(n * C, C)
        for t in range(0, C, T_MIX):
            part = pl.ds(n * C + t, T_MIX)
            r = scale[part, :]
            s = slope[part, :]
            for h in every:
                weighted = g[part, head(h)].astype(F32) * gains[:, h * HD : (h + 1) * HD]
                d = r * weighted - attended[part, head(h)] * s
                grad[part, head(h)] = d.astype(BF16)
        sums = [dot(q[rows, head(h)], grad[rows, head(h)], TN) for h in every]
        for h in every:
            total = inside[state_rows(n, h, heads), :] + sums[h]
            if n > 0:
                linked = docs[n : n + 1, :] == docs[n - 1 : n, :]
                inside[state_rows(n - 1, h, heads), :] = jnp.where(linked, total, 0.0)
            else:
                message[head(h), :] = total
    message[heads * HD :, :] = jnp.broadcast_to(-docs[0:1, :], (PAD, HD))


def store_blocks(n, slot, pairs, cols, sems):
    return [
        pltpu.make_async_copy(stage.at[slot], out.at[block(n), cols], sems.at[i, slot])
        for i, (stage, out) in enumerate(pairs)
    ]


def query_side(own, blocks, heads, after, k, v, q, attended, scale, gain, grad, low, scores, *rest):
    rest = rest[2:] if own else rest
    normed, query_grad, key_local, value_local, done, stage_n, stage_q, sems = rest
    off = half_start(own, heads * HD)
    cols = pl.ds(off, heads * HD)
    gains = gain[:, cols]
    pairs = ((stage_n, normed), (stage_q, query_grad))
    causal = causal_mask()
    every = range(heads)

    def step(n, carried):
        rows = block(n)
        r = scale[rows, :]
        ds = [grad[rows, head(h)] for h in every]
        raw = [dot(ds[h], v[rows, head(h)], NT) for h in every]
        gs = [jnp.where(causal, x, 0.0).astype(BF16) for x in raw]
        qg = [
            dot(ds[h], low[state_rows(n, h, heads), :], NT) + dot(gs[h], k[rows, head(h)], NN)
            for h in every
        ]
        kg = [dot(q[rows, head(h)], gs[h], TN).T for h in every]
        vg = [dot(ds[h], scores[score_rows(n, h, heads), :], TN).T for h in every]
        outs = [
            attended[rows, head(h)] * r * gains[:, h * HD : (h + 1) * HD] for h in every
        ]
        for h in every:
            stage_q[n, :, head(h)] = qg[h].astype(BF16)
            stage_n[n, :, head(h)] = outs[h].astype(BF16)
            key_local[rows, head(h)] = kg[h]
            value_local[rows, head(h)] = vg[h]
        for copy in store_blocks(n, n, pairs, cols, sems):
            copy.start()
        return carried

    lax.fori_loop(0, blocks, step, 0, unroll=U_Q)
    for n in range(blocks):
        for copy in store_blocks(n, n, pairs, cols, sems):
            copy.wait()
    done[...] = jnp.zeros(done.shape, F32)


def key_side(own, blocks, heads, docs, inside, carry, k, v, key_local, value_local, *rest):
    rest = rest if own else rest[2:]
    key_grad, value_grad, stage_k, stage_v, sems = rest
    off = half_start(own, heads * HD)
    cols = pl.ds(off, heads * HD)
    pairs = ((stage_k, key_grad), (stage_v, value_grad))
    every = range(heads)

    def step(n, carried):
        rows = block(n)
        hit = carry[heads * HD : heads * HD + 1, :] == -docs[pl.ds(n, 1), :]
        states = []
        for h in every:
            state = inside[state_rows(n, h, heads), :] + jnp.where(hit, carry[head(h), :], 0.0)
            states.append(state.astype(BF16))
        kg = [dot(v[rows, head(h)], states[h], NT) for h in every]
        vg = [dot(k[rows, head(h)], states[h], NN) for h in every]
        kg = [(kg[h] + key_local[rows, head(h)]).astype(BF16) for h in every]
        vg = [(vg[h] + value_local[rows, head(h)]).astype(BF16) for h in every]
        for h in every:
            stage_k[n, :, head(h)] = kg[h]
            stage_v[n, :, head(h)] = vg[h]
        for copy in store_blocks(n, n, pairs, cols, sems):
            copy.start()
        return carried

    lax.fori_loop(0, blocks, step, 0, unroll=U_K)
    for n in range(blocks):
        for copy in store_blocks(n, n, pairs, cols, sems):
            copy.wait()


def merge_kernel(reverse, outs, count, *refs):
    size = lax.axis_size("ctx")
    place = lax.axis_index("ctx")
    rank = size - 1 - place if reverse else place
    core = lax.rem(place, 2)

    def bit(b):
        return lax.rem(lax.div(rank, 1 << b), 2)

    ins, results = refs[:count], refs[count:]
    rows = results[0].shape[0] - PAD
    for terms, result in zip(outs, results):
        keys = []
        for source, flag in terms:
            key = ins[source][rows : rows + 1, :]
            keys.append(key if flag is None else jnp.where(flag(bit, core), key, NEVER))
        latest = functools.reduce(jnp.maximum, keys)
        parts = [
            jnp.where(key == latest, ins[source][:rows, :], 0.0)
            for (source, _), key in zip(terms, keys)
        ]
        result[:rows, :] = functools.reduce(jnp.add, parts)
        result[rows:, :] = jnp.broadcast_to(latest, (PAD, HD))


def merge(ins, outs, reverse, after=()):
    ins = list(ins) + list(after)
    return pl.pallas_call(
        functools.partial(merge_kernel, reverse, outs, len(ins)),
        name="merge",
        out_shape=[pltpu.VMEM(ins[0].shape, F32)] * len(outs),
        in_specs=[VM] * len(ins),
        out_specs=[VM] * len(outs),
        compiler_params=params(),
        cost_estimate=cost(0, 1 << 18),
    )(*ins)


def swap(message, even, odd):
    size = lax.axis_size("ctx")
    pairs = [(i, i ^ (1 << (odd if i % 2 else even))) for i in range(size)]
    return lax.ppermute(message, "ctx", pairs)


def scan(theirs, mine, reverse, first_work, second_work):
    top = lax.axis_size("ctx").bit_length() - 1
    lo, hi = top - 2, top - 1
    beside = swap(theirs, 0, 0)
    (total,) = merge([mine, beside], [[(0, None), (1, None)]], reverse)
    before = []
    for b in range(1, lo):
        got = swap(total, b, b)

        def is_high(bit, core, b=b):
            return bit(b) == 1

        earlier = [(2, None)] if before else []
        total, prior = merge(
            [total, got] + before,
            [[(0, None), (1, None)], [(1, is_high)] + earlier],
            reverse,
        )
        before = [prior]
    first = swap(total, lo, hi)
    first_done = first_work(total)
    (onward,) = merge(
        [total, first],
        [
            [
                (0, lambda bit, core: core * bit(lo) * bit(hi) == 0),
                (1, lambda bit, core: core * (1 - bit(hi)) == 0),
            ]
        ],
        reverse,
        first_done[-1:],
    )
    second = swap(onward, hi, lo)
    second_done = second_work(onward, first_done)

    def carried(neighbour, low_core):
        return [
            (0, lambda bit, core: (1 - core) * bit(lo) + core * bit(hi) == 1),
            (1, lambda bit, core: bit(hi) + core * bit(lo) > 0),
            (neighbour, lambda bit, core: bit(0) == low_core),
        ] + ([(4, None)] if before else [])

    carry_mine, carry_theirs = merge(
        [first, second, beside, mine] + before,
        [carried(2, 1), carried(3, 0)],
        reverse,
        second_done[-1:],
    )
    return carry_mine, swap(carry_theirs, 0, 0), first_done[:-1], second_done[:-1]


def local(queries, keys, values, out_grad, gain, doc_ids):
    tokens, features = queries.shape
    heads = features // HD // 2
    cols = heads * HD
    blocks = tokens // C
    lanes = -(-blocks // 8) * 8
    pairs = blocks * heads
    tp = lax.axis_size("tp")
    gain = gain.reshape(1, features)
    rows = cols + PAD
    narrow, wide, square = C * HD * HD, C * C * HD, HD * HD
    dma = pltpu.SemaphoreType.DMA
    half_bf = pltpu.VMEM((tokens, cols), BF16)
    half_f32 = pltpu.VMEM((tokens, cols), F32)
    states_f32 = pltpu.VMEM((pairs * HD, HD), F32)
    message = pltpu.VMEM((rows, HD), F32)
    whole = pltpu.HBM((tokens, features), BF16)
    column = pltpu.VMEM((tokens, HD), F32)

    keys, values, queries, out_grad, docs_hbm = [
        pltpu.with_memory_space_constraint(x, pltpu.HBM)
        for x in (keys, values, queries, out_grad, doc_ids)
    ]
    token = pltpu.VMEM((PAD, HD), F32)

    def states(own, k):
        ins = [k, docs_hbm, values] if own else [docs_hbm, keys, values]
        outs = [half_bf, states_f32, message]
        if not own:
            outs = [half_bf] + outs + [pltpu.VMEM((lanes, HD), F32), half_bf]
        return pl.pallas_call(
            functools.partial(key_value_states, own, blocks, heads),
            name=label("states", own),
            out_shape=outs,
            in_specs=[VM, HB, HB] if own else [HB, HB, HB],
            out_specs=[VM] * len(outs),
            scratch_shapes=[pltpu.SMEM((blocks,), jnp.int32), dma((2 * heads + 2,))],
            compiler_params=params(),
            cost_estimate=cost(2 * pairs * narrow, 4 * tokens * cols),
        )(*ins)

    def scoring(own, k, v, after):
        return pl.pallas_call(
            functools.partial(local_scores, own, blocks, heads),
            name=label("scoring", own),
            out_shape=[half_bf, half_bf, half_f32, pltpu.VMEM((pairs * C, C), BF16), token],
            in_specs=[VM] * 3 + [HB] * 2,
            out_specs=[VM] * 5,
            scratch_shapes=[dma((blocks,)), dma],
            compiler_params=params(),
            cost_estimate=cost(4 * pairs * wide, 4 * tokens * cols),
        )(after, k, v, queries, out_grad)

    def attending(own, inside, carry, q, sv, g, sums):
        ins = [docs, inside, carry, q, sv, g, gain] + ([] if own else [sums])
        last = [pltpu.VMEM((C, HD), F32)] if own else [pltpu.VMEM((2 * lanes, C), F32)]
        return pl.pallas_call(
            functools.partial(attend, own, blocks, heads, lanes),
            name=label("attend", own),
            out_shape=[half_f32, pltpu.VMEM((pairs * HD, HD), BF16)] + last,
            in_specs=[VM] * len(ins),
            out_specs=[VM] * 3,
            scratch_shapes=[] if own else [pltpu.VMEM((C, HD), F32)],
            compiler_params=params(),
            cost_estimate=cost(2 * pairs * narrow, 1 << 20),
        )(*ins)

    def mixing(own, before, attended, q, g):
        ins = [docs] + before + [attended, q, g, gain]
        outs = [half_bf, states_f32, message] + ([] if own else [column, column])
        return pl.pallas_call(
            functools.partial(mixed, own, blocks, heads, lanes, tp),
            name=label("mixed", own),
            out_shape=outs,
            in_specs=[VM] * len(ins),
            out_specs=[VM] * len(outs),
            scratch_shapes=[] if own else [pltpu.VMEM((HD, C), F32)],
            compiler_params=params(),
            cost_estimate=cost(2 * pairs * narrow, 1 << 20),
        )(*ins)

    def query_grads(own, k, v, q, attended, scale, grad, low, scores, so_far, after):
        ins = [after, k, v, q, attended, scale, gain, grad, low, scores] + list(so_far)
        stage = pltpu.VMEM((blocks, C, cols), BF16)
        return pl.pallas_call(
            functools.partial(query_side, own, blocks, heads),
            name=label("query_side", own),
            out_shape=[whole, whole, half_f32, half_f32, token],
            in_specs=[VM] * 10 + [HB] * len(so_far),
            out_specs=[HB, HB, VM, VM, VM],
            scratch_shapes=[stage, stage, dma((2, blocks))],
            input_output_aliases={10: 0, 11: 1} if own else {},
            compiler_params=params(),
            cost_estimate=cost(8 * pairs * wide, 4 * tokens * cols),
        )(*ins)

    def key_grads(own, inside, carry, k, v, key_local, value_local, so_far):
        ins = [docs, inside, carry, k, v, key_local, value_local] + list(so_far)
        stage = pltpu.VMEM((blocks, C, cols), BF16)
        return pl.pallas_call(
            functools.partial(key_side, own, blocks, heads),
            name=label("key_side", own),
            out_shape=[whole, whole],
            in_specs=[VM] * 7 + [HB] * len(so_far),
            out_specs=[HB, HB],
            scratch_shapes=[stage, stage, dma((2, blocks))],
            input_output_aliases={} if own else {7: 0, 8: 1},
            compiler_params=params(),
            cost_estimate=cost(4 * pairs * narrow, 4 * tokens * cols),
        )(*ins)

    k1, v1, inside1, theirs, docs, k0 = states(False, None)
    v0, inside0, mine = states(True, k0)
    carry0, carry1, (q1, g1, local1, scores1), (q0, g0, local0, scores0) = scan(
        theirs,
        mine,
        False,
        lambda after: scoring(False, k1, v1, after),
        lambda after, _: scoring(True, k0, v0, after),
    )
    att0, low0, sums = attending(True, inside0, carry0, q0, local0, g0, None)
    att1, low1, sums = attending(False, inside1, carry1, q1, local1, g1, sums)
    parts = [sums] + [
        lax.ppermute(sums, "tp", [(i, (i + s) % tp) for i in range(tp)]) for s in range(1, tp)
    ]
    grad1, after1, theirs, scale, slope = mixing(False, parts, att1, q1, g1)
    grad0, after0, mine = mixing(True, [scale, slope], att0, q0, g0)
    carry0, carry1, (_, _, kl1, vl1), (normed, query_grad, kl0, vl0) = scan(
        theirs,
        mine,
        True,
        lambda after: query_grads(False, k1, v1, q1, att1, scale, grad1, low1, scores1, (), after),
        lambda after, done: query_grads(
            True, k0, v0, q0, att0, scale, grad0, low0, scores0, done[:2], after
        ),
    )
    key_grad, value_grad = key_grads(True, after0, carry0, k0, v0, kl0, vl0, ())
    key_grad, value_grad = key_grads(
        False, after1, carry1, k1, v1, kl1, vl1, (key_grad, value_grad)
    )
    return normed, query_grad, key_grad, value_grad


def solution(mesh):
    return jax.shard_map(
        local,
        mesh=mesh,
        in_specs=(
            P("ctx", "tp"),
            P("ctx", "tp"),
            P("ctx", "tp"),
            P("ctx", "tp"),
            P("tp"),
            P("ctx"),
        ),
        out_specs=(P("ctx", "tp"), P("ctx", "tp"), P("ctx", "tp"), P("ctx", "tp")),
        check_vma=False,
    )
```

```python
import functools

import jax
import jax.numpy as jnp
from jax import lax
from jax.experimental import pallas as pl
from jax.experimental.pallas import tpu as pltpu
from jax.sharding import PartitionSpec as P

HD = 128
C = 256
QW = 4096
PAD = 8
NEVER = -1.0e9
MIB = 1 << 20
U_SCORE = 4
U_ATT = 6
U_Q = 6
U_K = 6
T_ATT = 128
T_MIX = 128

epsilon = 1e-06

F32 = jnp.float32
BF16 = jnp.bfloat16
VM = pl.BlockSpec(memory_space=pltpu.VMEM)
HB = pl.BlockSpec(memory_space=pltpu.HBM)


def dot(a, b, dims):
    return lax.dot_general(a, b, (dims, ((), ())), preferred_element_type=F32)


NN = ((1,), (0,))
NT = ((1,), (1,))
TN = ((0,), (0,))


def params(mib=12):
    return pltpu.CompilerParams(vmem_limit_bytes=mib * MIB)


def cost(flops, nbytes):
    return pl.CostEstimate(flops=int(flops), bytes_accessed=int(nbytes), transcendentals=0)


def half_start(own, cols):
    core = lax.rem(lax.axis_index("ctx"), 2)
    half = core if own else 1 - core
    return pl.multiple_of(half * cols, 128)


def label(name, own):
    return name + ("_own" if own else "_other")


def head(h):
    return pl.ds(h * HD, HD)


def block(n):
    return pl.ds(n * C if isinstance(n, int) else pl.multiple_of(n * C, C), C)


def state_rows(n, h, heads):
    start = (n * heads + h) * HD
    return pl.ds(start if isinstance(start, int) else pl.multiple_of(start, HD), HD)


def key_value_states(own, blocks, heads, *refs):
    if own:
        k, docs_hbm, v_hbm, v, inside, message, docs, sems = refs
    else:
        docs_hbm, k_hbm, v_hbm, k, v, inside, message, table, k_own, docs, sems = refs
    off = half_start(own, heads * HD)
    docs_copy = pltpu.make_async_copy(docs_hbm, docs, sems.at[2 * heads])
    width = 2 * HD if heads % 2 == 0 else HD
    groups = heads * HD // width
    copies = []
    for i in range(groups):
        src, dst = pl.ds(off + i * width, width), pl.ds(i * width, width)
        copies.append([pltpu.make_async_copy(v_hbm.at[:, src], v.at[:, dst], sems.at[2 * i])])
        if not own:
            copies[i].append(
                pltpu.make_async_copy(k_hbm.at[:, src], k.at[:, dst], sems.at[2 * i + 1])
            )
        for copy in copies[i]:
            copy.start()
    docs_copy.start()
    if not own:
        ahead = pltpu.make_async_copy(
            k_hbm.at[:, pl.ds(half_start(True, heads * HD), heads * HD)],
            k_own,
            sems.at[2 * heads + 1],
        )
        ahead.start()
    docs_copy.wait()
    for h in range(heads):
        if h * HD % width == 0:
            for copy in copies[h * HD // width]:
                copy.wait()
        per_block = [pl.ds(n * C, C) for n in range(blocks)]
        sums = [dot(k[rows, head(h)], v[rows, head(h)], TN) for rows in per_block]
        running = jnp.zeros((HD, HD), F32)
        for n in range(blocks):
            inside[state_rows(n, h, heads), :] = running
            total = running + sums[n]
            if n + 1 < blocks:
                running = jnp.where(docs[n] == docs[n + 1], total, 0.0)
            else:
                message[head(h), :] = total
    message[heads * HD :, :] = jnp.full((PAD, HD), docs[blocks - 1].astype(F32), F32)
    if not own:
        table[...] = jnp.zeros(table.shape, F32)
        for n in range(blocks):
            table[n : n + 1, :] = jnp.full((1, HD), docs[n].astype(F32), F32)
        ahead.wait()


def causal_mask():
    return lax.broadcasted_iota(jnp.int32, (C, C), 0) >= lax.broadcasted_iota(jnp.int32, (C, C), 1)


def score_rows(n, h, heads):
    start = (n * heads + h) * C
    return pl.ds(start if isinstance(start, int) else pl.multiple_of(start, C), C)


def local_scores(
    own, blocks, heads, after, k, v, gain, q_hbm, g_hbm, q, weighted, local, scores, done, g, sems
):
    off = half_start(own, heads * HD)
    gains = gain[:, pl.ds(off, heads * HD)]
    group = 2 if heads % 2 == 0 else 1
    copies = []
    for h in range(0, heads, group):
        src, dst = pl.ds(off + h * HD, group * HD), pl.ds(h * HD, group * HD)
        copies.append(pltpu.make_async_copy(q_hbm.at[:, src], q.at[:, dst], sems.at[h]))
        copies[-1].start()
    g_copy = pltpu.make_async_copy(g_hbm.at[:, pl.ds(off, heads * HD)], g, sems.at[heads])
    g_copy.start()
    causal = causal_mask()
    for h in range(0, heads, group):
        copies[h // group].wait()
        units = [(n, i) for n in range(blocks) for i in range(h, h + group)]
        for at in range(0, len(units), U_SCORE):
            now = units[at : at + U_SCORE]
            raw = [dot(q[block(n), head(i)], k[block(n), head(i)], NT) for n, i in now]
            low = [jnp.where(causal, s, 0.0).astype(BF16) for s in raw]
            outs = [dot(s, v[block(n), head(i)], NN) for s, (n, i) in zip(low, now)]
            for (n, i), s, out in zip(now, low, outs):
                scores[score_rows(n, i, heads), :] = s
                local[block(n), head(i)] = out
    g_copy.wait()
    for n in range(blocks):
        weighted[block(n), :] = g[block(n), :].astype(F32) * gains
    done[...] = jnp.zeros(done.shape, F32)


def attend(own, blocks, heads, lanes, docs, inside, carry, q, local, weighted, *rest):
    if own:
        attended, low, sums = rest
        sums[...] = jnp.zeros((C, HD), F32)
    else:
        sums_in, attended, low, message, sums = rest
        sums[...] = sums_in[...]
    lane = lax.broadcasted_iota(jnp.int32, (T_ATT, HD), 1)
    every = range(heads)

    def step(n, carried):
        hit = carry[heads * HD : heads * HD + 1, :] == docs[pl.ds(n, 1), :]
        states = []
        for h in every:
            state = inside[state_rows(n, h, heads), :] + jnp.where(hit, carry[head(h), :], 0.0)
            states.append(state.astype(BF16))
            low[state_rows(n, h, heads), :] = states[h]
        for t in range(0, C, T_ATT):
            rows = pl.ds(pl.multiple_of(n * C + t, T_ATT), T_ATT)
            square = jnp.zeros((T_ATT, HD), F32)
            inner = jnp.zeros((T_ATT, HD), F32)
            for h in every:
                out = local[rows, head(h)] + dot(q[rows, head(h)], states[h], NN)
                attended[rows, head(h)] = out
                square += out * out
                inner += weighted[rows, head(h)] * out
            square = jnp.sum(square, axis=1, keepdims=True)
            inner = jnp.sum(inner, axis=1, keepdims=True)
            sums[t : t + T_ATT, :] += jnp.where(lane == n, square, 0.0) + jnp.where(
                lane == n + lanes, inner, 0.0
            )
        return carried

    lax.fori_loop(0, blocks, step, 0, unroll=U_ATT)
    if not own:
        message[...] = jnp.transpose(sums[...])[: 2 * lanes, :]


def mixed(own, blocks, heads, lanes, parts, docs, *rest):
    if not own:
        pieces, rest = rest[:parts], rest[parts:]
        attended, q, weighted, grad, inside, message, scale, slope, turn = rest
        total = pieces[0][...]
        for piece in pieces[1:]:
            total = total + piece[...]
        r = lax.rsqrt(total[:lanes] / QW + epsilon)
        s = r * r * r * (total[lanes:] / QW)
        turn[...] = jnp.zeros((HD, C), F32)
        turn[:lanes, :] = r
        turn[lanes : 2 * lanes, :] = s
        columns = jnp.transpose(turn[...])
        for n in range(blocks):
            rows = pl.ds(n * C, C)
            scale[rows, :] = jnp.broadcast_to(columns[:, n : n + 1], (C, HD))
            slope[rows, :] = jnp.broadcast_to(columns[:, lanes + n : lanes + n + 1], (C, HD))
    else:
        scale, slope, attended, q, weighted, grad, inside, message = rest
    every = range(heads)
    for h in every:
        inside[state_rows(blocks - 1, h, heads), :] = jnp.zeros((HD, HD), F32)
    for n in reversed(range(blocks)):
        rows = pl.ds(n * C, C)
        for t in range(0, C, T_MIX):
            part = pl.ds(n * C + t, T_MIX)
            r = scale[part, :]
            s = slope[part, :]
            for h in every:
                d = r * weighted[part, head(h)] - attended[part, head(h)] * s
                grad[part, head(h)] = d.astype(BF16)
        sums = [dot(q[rows, head(h)], grad[rows, head(h)], TN) for h in every]
        for h in every:
            total = inside[state_rows(n, h, heads), :] + sums[h]
            if n > 0:
                linked = docs[n : n + 1, :] == docs[n - 1 : n, :]
                inside[state_rows(n - 1, h, heads), :] = jnp.where(linked, total, 0.0)
            else:
                message[head(h), :] = total
    message[heads * HD :, :] = jnp.broadcast_to(-docs[0:1, :], (PAD, HD))


def store_blocks(n, slot, pairs, cols, sems):
    return [
        pltpu.make_async_copy(stage.at[slot], out.at[block(n), cols], sems.at[i, slot])
        for i, (stage, out) in enumerate(pairs)
    ]


def query_side(own, blocks, heads, after, k, v, q, attended, scale, gain, grad, low, scores, *rest):
    rest = rest[2:] if own else rest
    normed, query_grad, key_local, value_local, done, stage_n, stage_q, sems = rest
    off = half_start(own, heads * HD)
    cols = pl.ds(off, heads * HD)
    gains = gain[:, cols]
    pairs = ((stage_n, normed), (stage_q, query_grad))
    causal = causal_mask()
    every = range(heads)

    def step(n, carried):
        rows = block(n)
        r = scale[rows, :]
        ds = [grad[rows, head(h)] for h in every]
        raw = [dot(ds[h], v[rows, head(h)], NT) for h in every]
        gs = [jnp.where(causal, x, 0.0).astype(BF16) for x in raw]
        qg = [
            dot(ds[h], low[state_rows(n, h, heads), :], NT) + dot(gs[h], k[rows, head(h)], NN)
            for h in every
        ]
        kg = [dot(q[rows, head(h)], gs[h], TN).T for h in every]
        vg = [dot(ds[h], scores[score_rows(n, h, heads), :], TN).T for h in every]
        outs = [
            attended[rows, head(h)] * r * gains[:, h * HD : (h + 1) * HD] for h in every
        ]
        for h in every:
            stage_q[n, :, head(h)] = qg[h].astype(BF16)
            stage_n[n, :, head(h)] = outs[h].astype(BF16)
            key_local[rows, head(h)] = kg[h]
            value_local[rows, head(h)] = vg[h]
        for copy in store_blocks(n, n, pairs, cols, sems):
            copy.start()
        return carried

    lax.fori_loop(0, blocks, step, 0, unroll=U_Q)
    for n in range(blocks):
        for copy in store_blocks(n, n, pairs, cols, sems):
            copy.wait()
    done[...] = jnp.zeros(done.shape, F32)


def key_side(own, blocks, heads, docs, inside, carry, k, v, key_local, value_local, *rest):
    rest = rest if own else rest[2:]
    key_grad, value_grad, stage_k, stage_v, sems = rest
    off = half_start(own, heads * HD)
    cols = pl.ds(off, heads * HD)
    pairs = ((stage_k, key_grad), (stage_v, value_grad))
    every = range(heads)

    def step(n, carried):
        rows = block(n)
        hit = carry[heads * HD : heads * HD + 1, :] == -docs[pl.ds(n, 1), :]
        states = []
        for h in every:
            state = inside[state_rows(n, h, heads), :] + jnp.where(hit, carry[head(h), :], 0.0)
            states.append(state.astype(BF16))
        kg = [dot(v[rows, head(h)], states[h], NT) for h in every]
        vg = [dot(k[rows, head(h)], states[h], NN) for h in every]
        kg = [(kg[h] + key_local[rows, head(h)]).astype(BF16) for h in every]
        vg = [(vg[h] + value_local[rows, head(h)]).astype(BF16) for h in every]
        for h in every:
            stage_k[n, :, head(h)] = kg[h]
            stage_v[n, :, head(h)] = vg[h]
        for copy in store_blocks(n, n, pairs, cols, sems):
            copy.start()
        return carried

    lax.fori_loop(0, blocks, step, 0, unroll=U_K)
    for n in range(blocks):
        for copy in store_blocks(n, n, pairs, cols, sems):
            copy.wait()


def merge_kernel(reverse, outs, count, *refs):
    size = lax.axis_size("ctx")
    place = lax.axis_index("ctx")
    rank = size - 1 - place if reverse else place
    core = lax.rem(place, 2)

    def bit(b):
        return lax.rem(lax.div(rank, 1 << b), 2)

    ins, results = refs[:count], refs[count:]
    for pieces, result in zip(outs, results):
        at = 0
        for rows, terms in pieces:
            keys = []
            for source, _, flag in terms:
                end = ins[source].shape[0] - PAD
                key = ins[source][end : end + 1, :]
                keys.append(key if flag is None else jnp.where(flag(bit, core), key, NEVER))
            latest = functools.reduce(jnp.maximum, keys)
            parts = [
                jnp.where(key == latest, ins[source][start : start + rows, :], 0.0)
                for (source, start, _), key in zip(terms, keys)
            ]
            result[at : at + rows, :] = functools.reduce(jnp.add, parts)
            at += rows
        result[at:, :] = jnp.broadcast_to(latest, (PAD, HD))


def merge(ins, outs, reverse, after=()):
    ins = list(ins) + list(after)
    shapes = [pltpu.VMEM((sum(rows for rows, _ in pieces) + PAD, HD), F32) for pieces in outs]
    return pl.pallas_call(
        functools.partial(merge_kernel, reverse, outs, len(ins)),
        name="merge",
        out_shape=shapes,
        in_specs=[VM] * len(ins),
        out_specs=[VM] * len(outs),
        compiler_params=params(),
        cost_estimate=cost(0, 1 << 18),
    )(*ins)


def swap(message, even, odd):
    size = lax.axis_size("ctx")
    pairs = [(i, i ^ (1 << (odd if i % 2 else even))) for i in range(size)]
    return lax.ppermute(message, "ctx", pairs)


def scan(theirs, mine, reverse, ways, first_work, second_work):
    rows = mine.shape[0] - PAD
    part = rows // ways
    every = range(ways)
    top = lax.axis_size("ctx").bit_length() - 1
    lo, hi = top - 2, top - 1

    def routed(way, flag):
        return lambda bit, core: flag(bit(lo), bit(hi), core if ways == 1 else way)

    def axes(way):
        return (lo, hi) if ways == 1 else ((lo, lo), (hi, hi))[way]

    beside = swap(theirs, 0, 0)
    totals = merge(
        [mine, beside],
        [[(part, [(0, w * part, None), (1, w * part, None)])] for w in every],
        reverse,
    )
    before = []
    for b in range(1, lo):
        got = [swap(totals[w], b, b) for w in every]

        def is_high(bit, core, b=b):
            return bit(b) == 1

        earlier = [[(2 * ways + w, 0, None)] if before else [] for w in every]
        both = merge(
            list(totals) + got + list(before),
            [[(part, [(w, 0, None), (ways + w, 0, None)])] for w in every]
            + [[(part, [(ways + w, 0, is_high)] + earlier[w])] for w in every],
            reverse,
        )
        totals, before = both[:ways], both[ways:]
    first = [swap(totals[w], *axes(w)) for w in every]
    first_done = first_work(totals[0])
    onward = [
        merge(
            [totals[w], first[w]],
            [
                [
                    (
                        part,
                        [
                            (0, 0, routed(w, lambda low, high, r: r * low * high == 0)),
                            (1, 0, routed(w, lambda low, high, r: r * (1 - high) == 0)),
                        ],
                    )
                ]
            ],
            reverse,
            first_done[-1:],
        )[0]
        for w in every
    ]
    second = [swap(onward[w], *axes(w)[::-1] if ways == 1 else axes(1 - w)) for w in every]
    second_done = second_work(onward[-1], first_done)

    def carried(neighbour, low_core):
        return [
            (
                part,
                [
                    (w, 0, routed(w, lambda low, high, r: (1 - r) * low + r * high == 1)),
                    (ways + w, 0, routed(w, lambda low, high, r: high + r * low > 0)),
                    (neighbour, w * part, lambda bit, core: bit(0) == low_core),
                ]
                + ([(2 * ways + 2 + w, 0, None)] if before else []),
            )
            for w in every
        ]

    carry_mine, carry_theirs = merge(
        first + second + [beside, mine] + list(before),
        [carried(2 * ways, 1), carried(2 * ways + 1, 0)],
        reverse,
        second_done[-1:],
    )
    return carry_mine, swap(carry_theirs, 0, 0), first_done[:-1], second_done[:-1]


def local(queries, keys, values, out_grad, gain, doc_ids):
    tokens, features = queries.shape
    heads = features // HD // 2
    cols = heads * HD
    blocks = tokens // C
    lanes = -(-blocks // 8) * 8
    pairs = blocks * heads
    tp = lax.axis_size("tp")
    gain = gain.reshape(1, features)
    rows = cols + PAD
    narrow, wide, square = C * HD * HD, C * C * HD, HD * HD
    dma = pltpu.SemaphoreType.DMA
    half_bf = pltpu.VMEM((tokens, cols), BF16)
    half_f32 = pltpu.VMEM((tokens, cols), F32)
    states_f32 = pltpu.VMEM((pairs * HD, HD), F32)
    message = pltpu.VMEM((rows, HD), F32)
    whole = pltpu.HBM((tokens, features), BF16)
    column = pltpu.VMEM((tokens, HD), F32)

    keys, values, queries, out_grad, docs_hbm = [
        pltpu.with_memory_space_constraint(x, pltpu.HBM)
        for x in (keys, values, queries, out_grad, doc_ids)
    ]
    token = pltpu.VMEM((PAD, HD), F32)

    def states(own, k):
        ins = [k, docs_hbm, values] if own else [docs_hbm, keys, values]
        outs = [half_bf, states_f32, message]
        if not own:
            outs = [half_bf] + outs + [pltpu.VMEM((lanes, HD), F32), half_bf]
        return pl.pallas_call(
            functools.partial(key_value_states, own, blocks, heads),
            name=label("states", own),
            out_shape=outs,
            in_specs=[VM, HB, HB] if own else [HB, HB, HB],
            out_specs=[VM] * len(outs),
            scratch_shapes=[pltpu.SMEM((blocks,), jnp.int32), dma((2 * heads + 2,))],
            compiler_params=params(),
            cost_estimate=cost(2 * pairs * narrow, 4 * tokens * cols),
        )(*ins)

    def scoring(own, k, v, after):
        return pl.pallas_call(
            functools.partial(local_scores, own, blocks, heads),
            name=label("scoring", own),
            out_shape=[half_bf, half_f32, half_f32, pltpu.VMEM((pairs * C, C), BF16), token],
            in_specs=[VM] * 4 + [HB] * 2,
            out_specs=[VM] * 5,
            scratch_shapes=[half_bf, dma((heads + 1,))],
            compiler_params=params(),
            cost_estimate=cost(4 * pairs * wide, 4 * tokens * cols),
        )(after, k, v, gain, queries, out_grad)

    def attending(own, inside, carry, q, sv, weighted, sums):
        ins = [docs, inside, carry, q, sv, weighted] + ([] if own else [sums])
        last = [pltpu.VMEM((C, HD), F32)] if own else [pltpu.VMEM((2 * lanes, C), F32)]
        return pl.pallas_call(
            functools.partial(attend, own, blocks, heads, lanes),
            name=label("attend", own),
            out_shape=[half_f32, pltpu.VMEM((pairs * HD, HD), BF16)] + last,
            in_specs=[VM] * len(ins),
            out_specs=[VM] * 3,
            scratch_shapes=[] if own else [pltpu.VMEM((C, HD), F32)],
            compiler_params=params(),
            cost_estimate=cost(2 * pairs * narrow, 1 << 20),
        )(*ins)

    def mixing(own, before, attended, q, weighted):
        ins = [docs] + before + [attended, q, weighted]
        outs = [half_bf, states_f32, message] + ([] if own else [column, column])
        return pl.pallas_call(
            functools.partial(mixed, own, blocks, heads, lanes, tp),
            name=label("mixed", own),
            out_shape=outs,
            in_specs=[VM] * len(ins),
            out_specs=[VM] * len(outs),
            scratch_shapes=[] if own else [pltpu.VMEM((HD, C), F32)],
            compiler_params=params(),
            cost_estimate=cost(2 * pairs * narrow, 1 << 20),
        )(*ins)

    def query_grads(own, k, v, q, attended, scale, grad, low, scores, so_far, after):
        ins = [after, k, v, q, attended, scale, gain, grad, low, scores] + list(so_far)
        stage = pltpu.VMEM((blocks, C, cols), BF16)
        return pl.pallas_call(
            functools.partial(query_side, own, blocks, heads),
            name=label("query_side", own),
            out_shape=[whole, whole, half_f32, half_f32, token],
            in_specs=[VM] * 10 + [HB] * len(so_far),
            out_specs=[HB, HB, VM, VM, VM],
            scratch_shapes=[stage, stage, dma((2, blocks))],
            input_output_aliases={10: 0, 11: 1} if own else {},
            compiler_params=params(),
            cost_estimate=cost(8 * pairs * wide, 4 * tokens * cols),
        )(*ins)

    def key_grads(own, inside, carry, k, v, key_local, value_local, so_far):
        ins = [docs, inside, carry, k, v, key_local, value_local] + list(so_far)
        stage = pltpu.VMEM((blocks, C, cols), BF16)
        return pl.pallas_call(
            functools.partial(key_side, own, blocks, heads),
            name=label("key_side", own),
            out_shape=[whole, whole],
            in_specs=[VM] * 7 + [HB] * len(so_far),
            out_specs=[HB, HB],
            scratch_shapes=[stage, stage, dma((2, blocks))],
            input_output_aliases={} if own else {7: 0, 8: 1},
            compiler_params=params(),
            cost_estimate=cost(4 * pairs * narrow, 4 * tokens * cols),
        )(*ins)

    k1, v1, inside1, theirs, docs, k0 = states(False, None)
    v0, inside0, mine = states(True, k0)
    carry0, carry1, (q1, w1, local1, scores1), (q0, w0, local0, scores0) = scan(
        theirs,
        mine,
        False,
        2,
        lambda after: scoring(False, k1, v1, after),
        lambda after, _: scoring(True, k0, v0, after),
    )
    att0, low0, sums = attending(True, inside0, carry0, q0, local0, w0, None)
    att1, low1, sums = attending(False, inside1, carry1, q1, local1, w1, sums)
    parts = [sums] + [
        lax.ppermute(sums, "tp", [(i, i ^ s) for i in range(tp)]) for s in range(1, tp)
    ]
    grad1, after1, theirs, scale, slope = mixing(False, parts, att1, q1, w1)
    grad0, after0, mine = mixing(True, [scale, slope], att0, q0, w0)
    carry0, carry1, (_, _, kl1, vl1), (normed, query_grad, kl0, vl0) = scan(
        theirs,
        mine,
        True,
        1,
        lambda after: query_grads(False, k1, v1, q1, att1, scale, grad1, low1, scores1, (), after),
        lambda after, done: query_grads(
            True, k0, v0, q0, att0, scale, grad0, low0, scores0, done[:2], after
        ),
    )
    key_grad, value_grad = key_grads(True, after0, carry0, k0, v0, kl0, vl0, ())
    key_grad, value_grad = key_grads(
        False, after1, carry1, k1, v1, kl1, vl1, (key_grad, value_grad)
    )
    return normed, query_grad, key_grad, value_grad


def solution(mesh):
    return jax.shard_map(
        local,
        mesh=mesh,
        in_specs=(
            P("ctx", "tp"),
            P("ctx", "tp"),
            P("ctx", "tp"),
            P("ctx", "tp"),
            P("tp"),
            P("ctx"),
        ),
        out_specs=(P("ctx", "tp"), P("ctx", "tp"), P("ctx", "tp"), P("ctx", "tp")),
        check_vma=False,
    )
```

```python
import functools

import jax
import jax.numpy as jnp
from jax import lax
from jax.experimental import pallas as pl
from jax.experimental.pallas import tpu as pltpu
from jax.sharding import PartitionSpec as P

HD = 128
C = 256
QW = 4096
PAD = 8
NEVER = -1.0e9
MIB = 1 << 20
U_SCORE = 4
U_ATT = 6
U_Q = 6
U_K = 6
T_ATT = 64
T_MIX = 128

epsilon = 1e-06

F32 = jnp.float32
BF16 = jnp.bfloat16
VM = pl.BlockSpec(memory_space=pltpu.VMEM)
HB = pl.BlockSpec(memory_space=pltpu.HBM)


def dot(a, b, dims):
    return lax.dot_general(a, b, (dims, ((), ())), preferred_element_type=F32)


NN = ((1,), (0,))
NT = ((1,), (1,))
TN = ((0,), (0,))


def params(mib=12):
    return pltpu.CompilerParams(vmem_limit_bytes=mib * MIB)


def cost(flops, nbytes):
    return pl.CostEstimate(flops=int(flops), bytes_accessed=int(nbytes), transcendentals=0)


def half_start(own, cols):
    core = lax.rem(lax.axis_index("ctx"), 2)
    half = core if own else 1 - core
    return pl.multiple_of(half * cols, 128)


def label(name, own):
    return name + ("_own" if own else "_other")


def head(h):
    return pl.ds(h * HD, HD)


def block(n):
    return pl.ds(n * C if isinstance(n, int) else pl.multiple_of(n * C, C), C)


def state_rows(n, h, heads):
    start = (n * heads + h) * HD
    return pl.ds(start if isinstance(start, int) else pl.multiple_of(start, HD), HD)


def key_value_states(own, blocks, heads, *refs):
    if own:
        k, _, docs_hbm, v_hbm, v, inside, message, docs, sems = refs
    else:
        docs_hbm, k_hbm, v_hbm, k, v, inside, message, table, k_own, v_own, docs, sems = refs
    off = half_start(own, heads * HD)
    docs_copy = pltpu.make_async_copy(docs_hbm, docs, sems.at[2 * heads])
    width = 2 * HD if heads % 2 == 0 else HD
    groups = heads * HD // width
    copies = [[] for _ in range(groups)]
    for i in range(1 if own else 0, groups):
        src, dst = pl.ds(off + i * width, width), pl.ds(i * width, width)
        copies[i].append(pltpu.make_async_copy(v_hbm.at[:, src], v.at[:, dst], sems.at[2 * i]))
        if not own:
            copies[i].append(
                pltpu.make_async_copy(k_hbm.at[:, src], k.at[:, dst], sems.at[2 * i + 1])
            )
        for copy in copies[i]:
            copy.start()
    docs_copy.start()
    ahead = []
    if not own:
        start = half_start(True, heads * HD)
        ahead = [
            pltpu.make_async_copy(
                k_hbm.at[:, pl.ds(start, heads * HD)], k_own, sems.at[2 * heads + 1]
            ),
            pltpu.make_async_copy(
                v_hbm.at[:, pl.ds(start, width)], v_own.at[:, :width], sems.at[2 * heads + 2]
            ),
        ]
        for copy in ahead:
            copy.start()
    docs_copy.wait()
    for h in range(heads):
        if h * HD % width == 0:
            for copy in copies[h * HD // width]:
                copy.wait()
        per_block = [pl.ds(n * C, C) for n in range(blocks)]
        sums = [dot(k[rows, head(h)], v[rows, head(h)], TN) for rows in per_block]
        running = jnp.zeros((HD, HD), F32)
        for n in range(blocks):
            inside[state_rows(n, h, heads), :] = running
            total = running + sums[n]
            if n + 1 < blocks:
                running = jnp.where(docs[n] == docs[n + 1], total, 0.0)
            else:
                message[head(h), :] = total
    message[heads * HD :, :] = jnp.full((PAD, HD), docs[blocks - 1].astype(F32), F32)
    if not own:
        table[...] = jnp.zeros(table.shape, F32)
        for n in range(blocks):
            table[n : n + 1, :] = jnp.full((1, HD), docs[n].astype(F32), F32)
        for copy in ahead:
            copy.wait()


def causal_mask():
    return lax.broadcasted_iota(jnp.int32, (C, C), 0) >= lax.broadcasted_iota(jnp.int32, (C, C), 1)


def score_rows(n, h, heads):
    start = (n * heads + h) * C
    return pl.ds(start if isinstance(start, int) else pl.multiple_of(start, C), C)


def local_scores(
    own, blocks, heads, after, k, v, gain, q_hbm, g_hbm, q, weighted, local, scores, done, g, sems
):
    off = half_start(own, heads * HD)
    gains = gain[:, pl.ds(off, heads * HD)]
    group = 2 if heads % 2 == 0 else 1
    copies = []
    for h in range(0, heads, group):
        src, dst = pl.ds(off + h * HD, group * HD), pl.ds(h * HD, group * HD)
        copies.append(pltpu.make_async_copy(q_hbm.at[:, src], q.at[:, dst], sems.at[h]))
        copies[-1].start()
    g_copy = pltpu.make_async_copy(g_hbm.at[:, pl.ds(off, heads * HD)], g, sems.at[heads])
    g_copy.start()
    causal = causal_mask()
    for h in range(0, heads, group):
        copies[h // group].wait()
        units = [(n, i) for n in range(blocks) for i in range(h, h + group)]
        for at in range(0, len(units), U_SCORE):
            now = units[at : at + U_SCORE]
            raw = [dot(q[block(n), head(i)], k[block(n), head(i)], NT) for n, i in now]
            low = [jnp.where(causal, s, 0.0).astype(BF16) for s in raw]
            outs = [dot(s, v[block(n), head(i)], NN) for s, (n, i) in zip(low, now)]
            for (n, i), s, out in zip(now, low, outs):
                scores[score_rows(n, i, heads), :] = s
                local[block(n), head(i)] = out
    g_copy.wait()
    for n in range(blocks):
        weighted[block(n), :] = g[block(n), :].astype(F32) * gains
    done[...] = jnp.zeros(done.shape, F32)


def attend(own, blocks, heads, lanes, docs, inside, carry, q, local, weighted, *rest):
    if own:
        attended, low, sums = rest
        sums[...] = jnp.zeros((C, HD), F32)
    else:
        sums_in, attended, low, message, sums = rest
        sums[...] = sums_in[...]
    lane = lax.broadcasted_iota(jnp.int32, (T_ATT, HD), 1)
    every = range(heads)

    def step(n, carried):
        hit = carry[heads * HD : heads * HD + 1, :] == docs[pl.ds(n, 1), :]
        states = []
        for h in every:
            state = inside[state_rows(n, h, heads), :] + jnp.where(hit, carry[head(h), :], 0.0)
            states.append(state.astype(BF16))
            low[state_rows(n, h, heads), :] = states[h]
        for t in range(0, C, T_ATT):
            rows = pl.ds(pl.multiple_of(n * C + t, T_ATT), T_ATT)
            square = jnp.zeros((T_ATT, HD), F32)
            inner = jnp.zeros((T_ATT, HD), F32)
            for h in every:
                out = local[rows, head(h)] + dot(q[rows, head(h)], states[h], NN)
                attended[rows, head(h)] = out
                square += out * out
                inner += weighted[rows, head(h)] * out
            square = jnp.sum(square, axis=1, keepdims=True)
            inner = jnp.sum(inner, axis=1, keepdims=True)
            sums[t : t + T_ATT, :] += jnp.where(lane == n, square, 0.0) + jnp.where(
                lane == n + lanes, inner, 0.0
            )
        return carried

    lax.fori_loop(0, blocks, step, 0, unroll=U_ATT)
    if not own:
        message[...] = jnp.transpose(sums[...])[: 2 * lanes, :]


def mixed(own, blocks, heads, lanes, parts, docs, *rest):
    if not own:
        pieces, rest = rest[:parts], rest[parts:]
        attended, q, weighted, grad, inside, message, scale, slope, turn = rest
        total = pieces[0][...]
        for piece in pieces[1:]:
            total = total + piece[...]
        r = lax.rsqrt(total[:lanes] / QW + epsilon)
        s = r * r * r * (total[lanes:] / QW)
        turn[...] = jnp.zeros((HD, C), F32)
        turn[:lanes, :] = r
        turn[lanes : 2 * lanes, :] = s
        columns = jnp.transpose(turn[...])
        for n in range(blocks):
            rows = pl.ds(n * C, C)
            scale[rows, :] = jnp.broadcast_to(columns[:, n : n + 1], (C, HD))
            slope[rows, :] = jnp.broadcast_to(columns[:, lanes + n : lanes + n + 1], (C, HD))
    else:
        scale, slope, attended, q, weighted, grad, inside, message = rest
    every = range(heads)
    for h in every:
        inside[state_rows(blocks - 1, h, heads), :] = jnp.zeros((HD, HD), F32)
    for n in reversed(range(blocks)):
        rows = pl.ds(n * C, C)
        for t in range(0, C, T_MIX):
            part = pl.ds(n * C + t, T_MIX)
            r = scale[part, :]
            s = slope[part, :]
            for h in every:
                d = r * weighted[part, head(h)] - attended[part, head(h)] * s
                grad[part, head(h)] = d.astype(BF16)
        sums = [dot(q[rows, head(h)], grad[rows, head(h)], TN) for h in every]
        for h in every:
            total = inside[state_rows(n, h, heads), :] + sums[h]
            if n > 0:
                linked = docs[n : n + 1, :] == docs[n - 1 : n, :]
                inside[state_rows(n - 1, h, heads), :] = jnp.where(linked, total, 0.0)
            else:
                message[head(h), :] = total
    message[heads * HD :, :] = jnp.broadcast_to(-docs[0:1, :], (PAD, HD))


def store_blocks(n, slot, pairs, cols, sems):
    return [
        pltpu.make_async_copy(stage.at[slot], out.at[block(n), cols], sems.at[i, slot])
        for i, (stage, out) in enumerate(pairs)
    ]


def query_side(own, blocks, heads, after, k, v, q, attended, scale, gain, grad, low, scores, *rest):
    rest = rest[2:] if own else rest
    normed, query_grad, key_local, value_local, done, stage_n, stage_q, sems = rest
    off = half_start(own, heads * HD)
    cols = pl.ds(off, heads * HD)
    gains = gain[:, cols]
    pairs = ((stage_n, normed), (stage_q, query_grad))
    causal = causal_mask()
    every = range(heads)

    def step(n, carried):
        rows = block(n)
        r = scale[rows, :]
        ds = [grad[rows, head(h)] for h in every]
        raw = [dot(ds[h], v[rows, head(h)], NT) for h in every]
        gs = [jnp.where(causal, x, 0.0).astype(BF16) for x in raw]
        qg = [
            dot(ds[h], low[state_rows(n, h, heads), :], NT) + dot(gs[h], k[rows, head(h)], NN)
            for h in every
        ]
        kg = [dot(q[rows, head(h)], gs[h], TN).T for h in every]
        vg = [dot(ds[h], scores[score_rows(n, h, heads), :], TN).T for h in every]
        outs = [
            attended[rows, head(h)] * r * gains[:, h * HD : (h + 1) * HD] for h in every
        ]
        for h in every:
            stage_q[n, :, head(h)] = qg[h].astype(BF16)
            stage_n[n, :, head(h)] = outs[h].astype(BF16)
            key_local[rows, head(h)] = kg[h]
            value_local[rows, head(h)] = vg[h]
        for copy in store_blocks(n, n, pairs, cols, sems):
            copy.start()
        return carried

    lax.fori_loop(0, blocks, step, 0, unroll=U_Q)
    for n in range(blocks):
        for copy in store_blocks(n, n, pairs, cols, sems):
            copy.wait()
    done[...] = jnp.zeros(done.shape, F32)


def key_side(own, blocks, heads, docs, inside, carry, k, v, key_local, value_local, *rest):
    rest = rest if own else rest[2:]
    key_grad, value_grad, stage_k, stage_v, sems = rest
    off = half_start(own, heads * HD)
    cols = pl.ds(off, heads * HD)
    pairs = ((stage_k, key_grad), (stage_v, value_grad))
    every = range(heads)

    def step(n, carried):
        rows = block(n)
        hit = carry[heads * HD : heads * HD + 1, :] == -docs[pl.ds(n, 1), :]
        states = []
        for h in every:
            state = inside[state_rows(n, h, heads), :] + jnp.where(hit, carry[head(h), :], 0.0)
            states.append(state.astype(BF16))
        kg = [dot(v[rows, head(h)], states[h], NT) for h in every]
        vg = [dot(k[rows, head(h)], states[h], NN) for h in every]
        kg = [(kg[h] + key_local[rows, head(h)]).astype(BF16) for h in every]
        vg = [(vg[h] + value_local[rows, head(h)]).astype(BF16) for h in every]
        for h in every:
            stage_k[n, :, head(h)] = kg[h]
            stage_v[n, :, head(h)] = vg[h]
        for copy in store_blocks(n, n, pairs, cols, sems):
            copy.start()
        return carried

    lax.fori_loop(0, blocks, step, 0, unroll=U_K)
    for n in range(blocks):
        for copy in store_blocks(n, n, pairs, cols, sems):
            copy.wait()


def merge_kernel(reverse, outs, count, *refs):
    size = lax.axis_size("ctx")
    place = lax.axis_index("ctx")
    rank = size - 1 - place if reverse else place
    core = lax.rem(place, 2)

    def bit(b):
        return lax.rem(lax.div(rank, 1 << b), 2)

    ins, results = refs[:count], refs[count:]
    for pieces, result in zip(outs, results):
        at = 0
        for rows, terms in pieces:
            keys = []
            for source, _, flag in terms:
                end = ins[source].shape[0] - PAD
                key = ins[source][end : end + 1, :]
                keys.append(key if flag is None else jnp.where(flag(bit, core), key, NEVER))
            latest = functools.reduce(jnp.maximum, keys)
            parts = [
                jnp.where(key == latest, ins[source][start : start + rows, :], 0.0)
                for (source, start, _), key in zip(terms, keys)
            ]
            result[at : at + rows, :] = functools.reduce(jnp.add, parts)
            at += rows
        result[at:, :] = jnp.broadcast_to(latest, (PAD, HD))


def merge(ins, outs, reverse, after=()):
    ins = list(ins) + list(after)
    shapes = [pltpu.VMEM((sum(rows for rows, _ in pieces) + PAD, HD), F32) for pieces in outs]
    return pl.pallas_call(
        functools.partial(merge_kernel, reverse, outs, len(ins)),
        name="merge",
        out_shape=shapes,
        in_specs=[VM] * len(ins),
        out_specs=[VM] * len(outs),
        compiler_params=params(),
        cost_estimate=cost(0, 1 << 18),
    )(*ins)


def swap(message, even, odd):
    size = lax.axis_size("ctx")
    pairs = [(i, i ^ (1 << (odd if i % 2 else even))) for i in range(size)]
    return lax.ppermute(message, "ctx", pairs)


def scan(theirs, mine, reverse, ways, first_work, second_work):
    rows = mine.shape[0] - PAD
    part = rows // ways
    every = range(ways)
    top = lax.axis_size("ctx").bit_length() - 1
    lo, hi = top - 2, top - 1

    def routed(way, flag):
        return lambda bit, core: flag(bit(lo), bit(hi), core if ways == 1 else way)

    def axes(way):
        return (lo, hi) if ways == 1 else ((lo, lo), (hi, hi))[way]

    beside = swap(theirs, 0, 0)
    totals = merge(
        [mine, beside],
        [[(part, [(0, w * part, None), (1, w * part, None)])] for w in every],
        reverse,
    )
    before = []
    for b in range(1, lo):
        got = [swap(totals[w], b, b) for w in every]

        def is_high(bit, core, b=b):
            return bit(b) == 1

        earlier = [[(2 * ways + w, 0, None)] if before else [] for w in every]
        both = merge(
            list(totals) + got + list(before),
            [[(part, [(w, 0, None), (ways + w, 0, None)])] for w in every]
            + [[(part, [(ways + w, 0, is_high)] + earlier[w])] for w in every],
            reverse,
        )
        totals, before = both[:ways], both[ways:]
    first = [swap(totals[w], *axes(w)) for w in every]
    first_done = first_work(totals[0])
    onward = [
        merge(
            [totals[w], first[w]],
            [
                [
                    (
                        part,
                        [
                            (0, 0, routed(w, lambda low, high, r: r * low * high == 0)),
                            (1, 0, routed(w, lambda low, high, r: r * (1 - high) == 0)),
                        ],
                    )
                ]
            ],
            reverse,
            first_done[-1:],
        )[0]
        for w in every
    ]
    second = [swap(onward[w], *axes(w)[::-1] if ways == 1 else axes(1 - w)) for w in every]
    second_done = second_work(onward[-1], first_done)

    def carried(neighbour, low_core):
        return [
            (
                part,
                [
                    (w, 0, routed(w, lambda low, high, r: (1 - r) * low + r * high == 1)),
                    (ways + w, 0, routed(w, lambda low, high, r: high + r * low > 0)),
                    (neighbour, w * part, lambda bit, core: bit(0) == low_core),
                ]
                + ([(2 * ways + 2 + w, 0, None)] if before else []),
            )
            for w in every
        ]

    carry_mine, carry_theirs = merge(
        first + second + [beside, mine] + list(before),
        [carried(2 * ways, 1), carried(2 * ways + 1, 0)],
        reverse,
        second_done[-1:],
    )
    return carry_mine, swap(carry_theirs, 0, 0), first_done[:-1], second_done[:-1]


def local(queries, keys, values, out_grad, gain, doc_ids):
    tokens, features = queries.shape
    heads = features // HD // 2
    cols = heads * HD
    blocks = tokens // C
    lanes = -(-blocks // 8) * 8
    pairs = blocks * heads
    tp = lax.axis_size("tp")
    gain = gain.reshape(1, features)
    rows = cols + PAD
    narrow, wide, square = C * HD * HD, C * C * HD, HD * HD
    dma = pltpu.SemaphoreType.DMA
    half_bf = pltpu.VMEM((tokens, cols), BF16)
    half_f32 = pltpu.VMEM((tokens, cols), F32)
    states_f32 = pltpu.VMEM((pairs * HD, HD), F32)
    message = pltpu.VMEM((rows, HD), F32)
    whole = pltpu.HBM((tokens, features), BF16)
    column = pltpu.VMEM((tokens, HD), F32)

    keys, values, queries, out_grad, docs_hbm = [
        pltpu.with_memory_space_constraint(x, pltpu.HBM)
        for x in (keys, values, queries, out_grad, doc_ids)
    ]
    token = pltpu.VMEM((PAD, HD), F32)

    def states(own, ahead):
        ins = ahead + ([docs_hbm, values] if own else [docs_hbm, keys, values])
        outs = [half_bf, states_f32, message]
        if not own:
            outs = [half_bf] + outs + [pltpu.VMEM((lanes, HD), F32), half_bf, half_bf]
        return pl.pallas_call(
            functools.partial(key_value_states, own, blocks, heads),
            name=label("states", own),
            out_shape=outs,
            in_specs=[VM] * len(ahead) + [HB] * (len(ins) - len(ahead)),
            out_specs=[VM] * len(outs),
            scratch_shapes=[pltpu.SMEM((blocks,), jnp.int32), dma((2 * heads + 3,))],
            input_output_aliases={1: 0} if own else {},
            compiler_params=params(),
            cost_estimate=cost(2 * pairs * narrow, 4 * tokens * cols),
        )(*ins)

    def scoring(own, k, v, after):
        return pl.pallas_call(
            functools.partial(local_scores, own, blocks, heads),
            name=label("scoring", own),
            out_shape=[half_bf, half_f32, half_f32, pltpu.VMEM((pairs * C, C), BF16), token],
            in_specs=[VM] * 4 + [HB] * 2,
            out_specs=[VM] * 5,
            scratch_shapes=[half_bf, dma((heads + 1,))],
            compiler_params=params(),
            cost_estimate=cost(4 * pairs * wide, 4 * tokens * cols),
        )(after, k, v, gain, queries, out_grad)

    def attending(own, inside, carry, q, sv, weighted, sums):
        ins = [docs, inside, carry, q, sv, weighted] + ([] if own else [sums])
        last = [pltpu.VMEM((C, HD), F32)] if own else [pltpu.VMEM((2 * lanes, C), F32)]
        return pl.pallas_call(
            functools.partial(attend, own, blocks, heads, lanes),
            name=label("attend", own),
            out_shape=[half_f32, pltpu.VMEM((pairs * HD, HD), BF16)] + last,
            in_specs=[VM] * len(ins),
            out_specs=[VM] * 3,
            scratch_shapes=[] if own else [pltpu.VMEM((C, HD), F32)],
            compiler_params=params(),
            cost_estimate=cost(2 * pairs * narrow, 1 << 20),
        )(*ins)

    def mixing(own, before, attended, q, weighted):
        ins = [docs] + before + [attended, q, weighted]
        outs = [half_bf, states_f32, message] + ([] if own else [column, column])
        return pl.pallas_call(
            functools.partial(mixed, own, blocks, heads, lanes, tp),
            name=label("mixed", own),
            out_shape=outs,
            in_specs=[VM] * len(ins),
            out_specs=[VM] * len(outs),
            scratch_shapes=[] if own else [pltpu.VMEM((HD, C), F32)],
            compiler_params=params(),
            cost_estimate=cost(2 * pairs * narrow, 1 << 20),
        )(*ins)

    def query_grads(own, k, v, q, attended, scale, grad, low, scores, so_far, after):
        ins = [after, k, v, q, attended, scale, gain, grad, low, scores] + list(so_far)
        stage = pltpu.VMEM((blocks, C, cols), BF16)
        return pl.pallas_call(
            functools.partial(query_side, own, blocks, heads),
            name=label("query_side", own),
            out_shape=[whole, whole, half_f32, half_f32, token],
            in_specs=[VM] * 10 + [HB] * len(so_far),
            out_specs=[HB, HB, VM, VM, VM],
            scratch_shapes=[stage, stage, dma((2, blocks))],
            input_output_aliases={10: 0, 11: 1} if own else {},
            compiler_params=params(),
            cost_estimate=cost(8 * pairs * wide, 4 * tokens * cols),
        )(*ins)

    def key_grads(own, inside, carry, k, v, key_local, value_local, so_far):
        ins = [docs, inside, carry, k, v, key_local, value_local] + list(so_far)
        stage = pltpu.VMEM((blocks, C, cols), BF16)
        return pl.pallas_call(
            functools.partial(key_side, own, blocks, heads),
            name=label("key_side", own),
            out_shape=[whole, whole],
            in_specs=[VM] * 7 + [HB] * len(so_far),
            out_specs=[HB, HB],
            scratch_shapes=[stage, stage, dma((2, blocks))],
            input_output_aliases={} if own else {7: 0, 8: 1},
            compiler_params=params(),
            cost_estimate=cost(4 * pairs * narrow, 4 * tokens * cols),
        )(*ins)

    k1, v1, inside1, theirs, docs, k0, v0 = states(False, [])
    v0, inside0, mine = states(True, [k0, v0])
    carry0, carry1, (q1, w1, local1, scores1), (q0, w0, local0, scores0) = scan(
        theirs,
        mine,
        False,
        2,
        lambda after: scoring(False, k1, v1, after),
        lambda after, _: scoring(True, k0, v0, after),
    )
    att0, low0, sums = attending(True, inside0, carry0, q0, local0, w0, None)
    att1, low1, sums = attending(False, inside1, carry1, q1, local1, w1, sums)
    parts = [sums] + [
        lax.ppermute(sums, "tp", [(i, i ^ s) for i in range(tp)]) for s in range(1, tp)
    ]
    grad1, after1, theirs, scale, slope = mixing(False, parts, att1, q1, w1)
    grad0, after0, mine = mixing(True, [scale, slope], att0, q0, w0)
    carry0, carry1, (_, _, kl1, vl1), (normed, query_grad, kl0, vl0) = scan(
        theirs,
        mine,
        True,
        1,
        lambda after: query_grads(False, k1, v1, q1, att1, scale, grad1, low1, scores1, (), after),
        lambda after, done: query_grads(
            True, k0, v0, q0, att0, scale, grad0, low0, scores0, done[:2], after
        ),
    )
    key_grad, value_grad = key_grads(True, after0, carry0, k0, v0, kl0, vl0, ())
    key_grad, value_grad = key_grads(
        False, after1, carry1, k1, v1, kl1, vl1, (key_grad, value_grad)
    )
    return normed, query_grad, key_grad, value_grad


def solution(mesh):
    return jax.shard_map(
        local,
        mesh=mesh,
        in_specs=(
            P("ctx", "tp"),
            P("ctx", "tp"),
            P("ctx", "tp"),
            P("ctx", "tp"),
            P("tp"),
            P("ctx"),
        ),
        out_specs=(P("ctx", "tp"), P("ctx", "tp"), P("ctx", "tp"), P("ctx", "tp")),
        check_vma=False,
    )
```

```python
import functools

import jax
import jax.numpy as jnp
from jax import lax
from jax.experimental import pallas as pl
from jax.experimental.pallas import tpu as pltpu
from jax.sharding import PartitionSpec as P

HD = 128
C = 256
QW = 4096
PAD = 8
NEVER = -1.0e9
MIB = 1 << 20
U_SCORE = 4
U_ATT = 6
U_Q = 6
U_K = 6
T_ATT = 64
T_MIX = 128

epsilon = 1e-06

F32 = jnp.float32
BF16 = jnp.bfloat16
VM = pl.BlockSpec(memory_space=pltpu.VMEM)
HB = pl.BlockSpec(memory_space=pltpu.HBM)


def dot(a, b, dims):
    return lax.dot_general(a, b, (dims, ((), ())), preferred_element_type=F32)


NN = ((1,), (0,))
NT = ((1,), (1,))
TN = ((0,), (0,))


def params(mib=12):
    return pltpu.CompilerParams(vmem_limit_bytes=mib * MIB)


def cost(flops, nbytes):
    return pl.CostEstimate(flops=int(flops), bytes_accessed=int(nbytes), transcendentals=0)


def half_start(own, cols):
    core = lax.rem(lax.axis_index("ctx"), 2)
    half = core if own else 1 - core
    return pl.multiple_of(half * cols, 128)


def label(name, own):
    return name + ("_own" if own else "_other")


def head(h):
    return pl.ds(h * HD, HD)


def block(n):
    return pl.ds(n * C if isinstance(n, int) else pl.multiple_of(n * C, C), C)


def state_rows(n, h, heads):
    start = (n * heads + h) * HD
    return pl.ds(start if isinstance(start, int) else pl.multiple_of(start, HD), HD)


def key_value_states(own, blocks, heads, *refs):
    if own:
        k, _, docs_hbm, v_hbm, v, inside, message, docs, sems = refs
    else:
        docs_hbm, k_hbm, v_hbm, k, v, inside, message, table, k_own, v_own, docs, sems = refs
    off = half_start(own, heads * HD)
    docs_copy = pltpu.make_async_copy(docs_hbm, docs, sems.at[2 * heads])
    width = 2 * HD if heads % 2 == 0 else HD
    groups = heads * HD // width
    copies = [[] for _ in range(groups)]
    for i in range(1 if own else 0, groups):
        src, dst = pl.ds(off + i * width, width), pl.ds(i * width, width)
        copies[i].append(pltpu.make_async_copy(v_hbm.at[:, src], v.at[:, dst], sems.at[2 * i]))
        if not own:
            copies[i].append(
                pltpu.make_async_copy(k_hbm.at[:, src], k.at[:, dst], sems.at[2 * i + 1])
            )
        for copy in copies[i]:
            copy.start()
    docs_copy.start()
    ahead = []
    if not own:
        start = half_start(True, heads * HD)
        ahead = [
            pltpu.make_async_copy(
                k_hbm.at[:, pl.ds(start, heads * HD)], k_own, sems.at[2 * heads + 1]
            ),
            pltpu.make_async_copy(
                v_hbm.at[:, pl.ds(start, width)], v_own.at[:, :width], sems.at[2 * heads + 2]
            ),
        ]
        for copy in ahead:
            copy.start()
    docs_copy.wait()
    for h in range(heads):
        if h * HD % width == 0:
            for copy in copies[h * HD // width]:
                copy.wait()
        per_block = [pl.ds(n * C, C) for n in range(blocks)]
        sums = [dot(k[rows, head(h)], v[rows, head(h)], TN) for rows in per_block]
        running = jnp.zeros((HD, HD), F32)
        for n in range(blocks):
            inside[state_rows(n, h, heads), :] = running
            total = running + sums[n]
            if n + 1 < blocks:
                running = jnp.where(docs[n] == docs[n + 1], total, 0.0)
            else:
                message[head(h), :] = total
    message[heads * HD :, :] = jnp.full((PAD, HD), docs[blocks - 1].astype(F32), F32)
    if not own:
        table[...] = jnp.zeros(table.shape, F32)
        for n in range(blocks):
            table[n : n + 1, :] = jnp.full((1, HD), docs[n].astype(F32), F32)
        for copy in ahead:
            copy.wait()


def causal_mask():
    return lax.broadcasted_iota(jnp.int32, (C, C), 0) >= lax.broadcasted_iota(jnp.int32, (C, C), 1)


def score_rows(n, h, heads):
    start = (n * heads + h) * C
    return pl.ds(start if isinstance(start, int) else pl.multiple_of(start, C), C)


def local_scores(
    own, blocks, heads, after, k, v, gain, q_hbm, g_hbm, q, weighted, local, scores, done, g, sems
):
    off = half_start(own, heads * HD)
    gains = gain[:, pl.ds(off, heads * HD)]
    group = 2 if heads % 2 == 0 else 1
    copies = []
    for h in range(0, heads, group):
        src, dst = pl.ds(off + h * HD, group * HD), pl.ds(h * HD, group * HD)
        copies.append(pltpu.make_async_copy(q_hbm.at[:, src], q.at[:, dst], sems.at[h]))
        copies[-1].start()
    g_copy = pltpu.make_async_copy(g_hbm.at[:, pl.ds(off, heads * HD)], g, sems.at[heads])
    g_copy.start()
    causal = causal_mask()
    for h in range(0, heads, group):
        copies[h // group].wait()
        units = [(n, i) for n in range(blocks) for i in range(h, h + group)]
        for at in range(0, len(units), U_SCORE):
            now = units[at : at + U_SCORE]
            raw = [dot(q[block(n), head(i)], k[block(n), head(i)], NT) for n, i in now]
            low = [jnp.where(causal, s, 0.0).astype(BF16) for s in raw]
            outs = [dot(s, v[block(n), head(i)], NN) for s, (n, i) in zip(low, now)]
            for (n, i), s, out in zip(now, low, outs):
                scores[score_rows(n, i, heads), :] = s
                local[block(n), head(i)] = out
    g_copy.wait()
    for n in range(blocks):
        weighted[block(n), :] = g[block(n), :].astype(F32) * gains
    done[...] = jnp.zeros(done.shape, F32)


def attend(own, blocks, heads, lanes, docs, inside, carry, q, local, weighted, *rest):
    if own:
        attended, low, sums = rest
        sums[...] = jnp.zeros((C, HD), F32)
    else:
        sums_in, attended, low, message, sums = rest
        sums[...] = sums_in[...]
    lane = lax.broadcasted_iota(jnp.int32, (T_ATT, HD), 1)
    every = range(heads)

    def step(n, carried):
        hit = carry[heads * HD : heads * HD + 1, :] == docs[pl.ds(n, 1), :]
        states = []
        for h in every:
            state = inside[state_rows(n, h, heads), :] + jnp.where(hit, carry[head(h), :], 0.0)
            states.append(state.astype(BF16))
            low[state_rows(n, h, heads), :] = states[h]
        for t in range(0, C, T_ATT):
            rows = pl.ds(pl.multiple_of(n * C + t, T_ATT), T_ATT)
            square = jnp.zeros((T_ATT, HD), F32)
            inner = jnp.zeros((T_ATT, HD), F32)
            for h in every:
                out = local[rows, head(h)] + dot(q[rows, head(h)], states[h], NN)
                attended[rows, head(h)] = out
                square += out * out
                inner += weighted[rows, head(h)] * out
            square = jnp.sum(square, axis=1, keepdims=True)
            inner = jnp.sum(inner, axis=1, keepdims=True)
            sums[t : t + T_ATT, :] += jnp.where(lane == n, square, 0.0) + jnp.where(
                lane == n + lanes, inner, 0.0
            )
        return carried

    lax.fori_loop(0, blocks, step, 0, unroll=U_ATT)
    if not own:
        message[...] = jnp.transpose(sums[...])[: 2 * lanes, :]


def mixed(own, blocks, heads, lanes, parts, docs, *rest):
    if not own:
        pieces, rest = rest[:parts], rest[parts:]
        attended, q, weighted, grad, inside, message, scale, slope, turn = rest
        total = pieces[0][...]
        for piece in pieces[1:]:
            total = total + piece[...]
        r = lax.rsqrt(total[:lanes] / QW + epsilon)
        s = r * r * r * (total[lanes:] / QW)
        turn[...] = jnp.zeros((HD, C), F32)
        turn[:lanes, :] = r
        turn[lanes : 2 * lanes, :] = s
        columns = jnp.transpose(turn[...])
        for n in range(blocks):
            rows = pl.ds(n * C, C)
            scale[rows, :] = jnp.broadcast_to(columns[:, n : n + 1], (C, HD))
            slope[rows, :] = jnp.broadcast_to(columns[:, lanes + n : lanes + n + 1], (C, HD))
    else:
        scale, slope, attended, q, weighted, grad, inside, message = rest
    every = range(heads)
    for h in every:
        inside[state_rows(blocks - 1, h, heads), :] = jnp.zeros((HD, HD), F32)
    for n in reversed(range(blocks)):
        rows = pl.ds(n * C, C)
        for t in range(0, C, T_MIX):
            part = pl.ds(n * C + t, T_MIX)
            r = scale[part, :]
            s = slope[part, :]
            for h in every:
                d = r * weighted[part, head(h)] - attended[part, head(h)] * s
                grad[part, head(h)] = d.astype(BF16)
        if own and heads % 2 == 0:
            sums = []
            for h in range(0, heads, 2):
                both = pl.ds(h * HD, 2 * HD)
                square = dot(q[rows, both], grad[rows, both], TN)
                sums += [square[:HD, :HD], square[HD:, HD:]]
        else:
            sums = [dot(q[rows, head(h)], grad[rows, head(h)], TN) for h in every]
        for h in every:
            total = inside[state_rows(n, h, heads), :] + sums[h]
            if n > 0:
                linked = docs[n : n + 1, :] == docs[n - 1 : n, :]
                inside[state_rows(n - 1, h, heads), :] = jnp.where(linked, total, 0.0)
            else:
                message[head(h), :] = total
    message[heads * HD :, :] = jnp.broadcast_to(-docs[0:1, :], (PAD, HD))


def store_blocks(n, slot, pairs, cols, sems):
    return [
        pltpu.make_async_copy(stage.at[slot], out.at[block(n), cols], sems.at[i, slot])
        for i, (stage, out) in enumerate(pairs)
    ]


def query_side(own, blocks, heads, after, k, v, q, attended, scale, gain, grad, low, scores, *rest):
    rest = rest[2:] if own else rest
    normed, query_grad, key_local, value_local, done, stage_n, stage_q, sems = rest
    off = half_start(own, heads * HD)
    cols = pl.ds(off, heads * HD)
    gains = gain[:, cols]
    pairs = ((stage_n, normed), (stage_q, query_grad))
    causal = causal_mask()
    every = range(heads)

    def step(n, carried):
        rows = block(n)
        r = scale[rows, :]
        ds = [grad[rows, head(h)] for h in every]
        raw = [dot(ds[h], v[rows, head(h)], NT) for h in every]
        gs = [jnp.where(causal, x, 0.0).astype(BF16) for x in raw]
        qg = [
            dot(ds[h], low[state_rows(n, h, heads), :], NT) + dot(gs[h], k[rows, head(h)], NN)
            for h in every
        ]
        kg = [dot(q[rows, head(h)], gs[h], TN).T for h in every]
        vg = [dot(ds[h], scores[score_rows(n, h, heads), :], TN).T for h in every]
        outs = [
            attended[rows, head(h)] * r * gains[:, h * HD : (h + 1) * HD] for h in every
        ]
        for h in every:
            stage_q[n, :, head(h)] = qg[h].astype(BF16)
            stage_n[n, :, head(h)] = outs[h].astype(BF16)
            key_local[rows, head(h)] = kg[h]
            value_local[rows, head(h)] = vg[h]
        for copy in store_blocks(n, n, pairs, cols, sems):
            copy.start()
        return carried

    lax.fori_loop(0, blocks, step, 0, unroll=U_Q)
    for n in range(blocks):
        for copy in store_blocks(n, n, pairs, cols, sems):
            copy.wait()
    done[...] = jnp.zeros(done.shape, F32)


def key_side(own, blocks, heads, docs, inside, carry, k, v, key_local, value_local, *rest):
    rest = rest if own else rest[2:]
    key_grad, value_grad, stage_k, stage_v, sems = rest
    off = half_start(own, heads * HD)
    cols = pl.ds(off, heads * HD)
    pairs = ((stage_k, key_grad), (stage_v, value_grad))
    every = range(heads)

    def step(n, carried):
        rows = block(n)
        hit = carry[heads * HD : heads * HD + 1, :] == -docs[pl.ds(n, 1), :]
        states = []
        for h in every:
            state = inside[state_rows(n, h, heads), :] + jnp.where(hit, carry[head(h), :], 0.0)
            states.append(state.astype(BF16))
        kg = [dot(v[rows, head(h)], states[h], NT) for h in every]
        vg = [dot(k[rows, head(h)], states[h], NN) for h in every]
        kg = [(kg[h] + key_local[rows, head(h)]).astype(BF16) for h in every]
        vg = [(vg[h] + value_local[rows, head(h)]).astype(BF16) for h in every]
        for h in every:
            stage_k[n, :, head(h)] = kg[h]
            stage_v[n, :, head(h)] = vg[h]
        for copy in store_blocks(n, n, pairs, cols, sems):
            copy.start()
        return carried

    lax.fori_loop(0, blocks, step, 0, unroll=U_K)
    for n in range(blocks):
        for copy in store_blocks(n, n, pairs, cols, sems):
            copy.wait()


def merge_kernel(reverse, outs, count, *refs):
    size = lax.axis_size("ctx")
    place = lax.axis_index("ctx")
    rank = size - 1 - place if reverse else place
    core = lax.rem(place, 2)

    def bit(b):
        return lax.rem(lax.div(rank, 1 << b), 2)

    ins, results = refs[:count], refs[count:]
    for pieces, result in zip(outs, results):
        at = 0
        for rows, terms in pieces:
            keys = []
            for source, _, flag in terms:
                end = ins[source].shape[0] - PAD
                key = ins[source][end : end + 1, :]
                keys.append(key if flag is None else jnp.where(flag(bit, core), key, NEVER))
            latest = functools.reduce(jnp.maximum, keys)
            parts = [
                jnp.where(key == latest, ins[source][start : start + rows, :], 0.0)
                for (source, start, _), key in zip(terms, keys)
            ]
            result[at : at + rows, :] = functools.reduce(jnp.add, parts)
            at += rows
        result[at:, :] = jnp.broadcast_to(latest, (PAD, HD))


def merge(ins, outs, reverse, after=()):
    ins = list(ins) + list(after)
    shapes = [pltpu.VMEM((sum(rows for rows, _ in pieces) + PAD, HD), F32) for pieces in outs]
    return pl.pallas_call(
        functools.partial(merge_kernel, reverse, outs, len(ins)),
        name="merge",
        out_shape=shapes,
        in_specs=[VM] * len(ins),
        out_specs=[VM] * len(outs),
        compiler_params=params(),
        cost_estimate=cost(0, 1 << 18),
    )(*ins)


def swap(message, even, odd):
    size = lax.axis_size("ctx")
    pairs = [(i, i ^ (1 << (odd if i % 2 else even))) for i in range(size)]
    return lax.ppermute(message, "ctx", pairs)


def scan(theirs, mine, reverse, ways, first_work, second_work):
    rows = mine.shape[0] - PAD
    part = rows // ways
    every = range(ways)
    top = lax.axis_size("ctx").bit_length() - 1
    lo, hi = top - 2, top - 1

    def routed(way, flag):
        return lambda bit, core: flag(bit(lo), bit(hi), core if ways == 1 else way)

    def axes(way):
        return (lo, hi) if ways == 1 else ((lo, lo), (hi, hi))[way]

    beside = swap(theirs, 0, 0)
    totals = merge(
        [mine, beside],
        [[(part, [(0, w * part, None), (1, w * part, None)])] for w in every],
        reverse,
    )
    before = []
    for b in range(1, lo):
        got = [swap(totals[w], b, b) for w in every]

        def is_high(bit, core, b=b):
            return bit(b) == 1

        earlier = [[(2 * ways + w, 0, None)] if before else [] for w in every]
        both = merge(
            list(totals) + got + list(before),
            [[(part, [(w, 0, None), (ways + w, 0, None)])] for w in every]
            + [[(part, [(ways + w, 0, is_high)] + earlier[w])] for w in every],
            reverse,
        )
        totals, before = both[:ways], both[ways:]
    first = [swap(totals[w], *axes(w)) for w in every]
    first_done = first_work(totals[0])
    onward = [
        merge(
            [totals[w], first[w]],
            [
                [
                    (
                        part,
                        [
                            (0, 0, routed(w, lambda low, high, r: r * low * high == 0)),
                            (1, 0, routed(w, lambda low, high, r: r * (1 - high) == 0)),
                        ],
                    )
                ]
            ],
            reverse,
            first_done[-1:],
        )[0]
        for w in every
    ]
    second = [swap(onward[w], *axes(w)[::-1] if ways == 1 else axes(1 - w)) for w in every]
    second_done = second_work(onward[-1], first_done)

    def carried(neighbour, low_core):
        return [
            (
                part,
                [
                    (w, 0, routed(w, lambda low, high, r: (1 - r) * low + r * high == 1)),
                    (ways + w, 0, routed(w, lambda low, high, r: high + r * low > 0)),
                    (neighbour, w * part, lambda bit, core: bit(0) == low_core),
                ]
                + ([(2 * ways + 2 + w, 0, None)] if before else []),
            )
            for w in every
        ]

    carry_mine, carry_theirs = merge(
        first + second + [beside, mine] + list(before),
        [carried(2 * ways, 1), carried(2 * ways + 1, 0)],
        reverse,
        second_done[-1:],
    )
    return carry_mine, swap(carry_theirs, 0, 0), first_done[:-1], second_done[:-1]


def local(queries, keys, values, out_grad, gain, doc_ids):
    tokens, features = queries.shape
    heads = features // HD // 2
    cols = heads * HD
    blocks = tokens // C
    lanes = -(-blocks // 8) * 8
    pairs = blocks * heads
    tp = lax.axis_size("tp")
    gain = gain.reshape(1, features)
    rows = cols + PAD
    narrow, wide, square = C * HD * HD, C * C * HD, HD * HD
    dma = pltpu.SemaphoreType.DMA
    half_bf = pltpu.VMEM((tokens, cols), BF16)
    half_f32 = pltpu.VMEM((tokens, cols), F32)
    states_f32 = pltpu.VMEM((pairs * HD, HD), F32)
    message = pltpu.VMEM((rows, HD), F32)
    whole = pltpu.HBM((tokens, features), BF16)
    column = pltpu.VMEM((tokens, HD), F32)

    keys, values, queries, out_grad, docs_hbm = [
        pltpu.with_memory_space_constraint(x, pltpu.HBM)
        for x in (keys, values, queries, out_grad, doc_ids)
    ]
    token = pltpu.VMEM((PAD, HD), F32)

    def states(own, ahead):
        ins = ahead + ([docs_hbm, values] if own else [docs_hbm, keys, values])
        outs = [half_bf, states_f32, message]
        if not own:
            outs = [half_bf] + outs + [pltpu.VMEM((lanes, HD), F32), half_bf, half_bf]
        return pl.pallas_call(
            functools.partial(key_value_states, own, blocks, heads),
            name=label("states", own),
            out_shape=outs,
            in_specs=[VM] * len(ahead) + [HB] * (len(ins) - len(ahead)),
            out_specs=[VM] * len(outs),
            scratch_shapes=[pltpu.SMEM((blocks,), jnp.int32), dma((2 * heads + 3,))],
            input_output_aliases={1: 0} if own else {},
            compiler_params=params(),
            cost_estimate=cost(2 * pairs * narrow, 4 * tokens * cols),
        )(*ins)

    def scoring(own, k, v, after):
        return pl.pallas_call(
            functools.partial(local_scores, own, blocks, heads),
            name=label("scoring", own),
            out_shape=[half_bf, half_f32, half_f32, pltpu.VMEM((pairs * C, C), BF16), token],
            in_specs=[VM] * 4 + [HB] * 2,
            out_specs=[VM] * 5,
            scratch_shapes=[half_bf, dma((heads + 1,))],
            compiler_params=params(),
            cost_estimate=cost(4 * pairs * wide, 4 * tokens * cols),
        )(after, k, v, gain, queries, out_grad)

    def attending(own, inside, carry, q, sv, weighted, sums):
        ins = [docs, inside, carry, q, sv, weighted] + ([] if own else [sums])
        last = [pltpu.VMEM((C, HD), F32)] if own else [pltpu.VMEM((2 * lanes, C), F32)]
        return pl.pallas_call(
            functools.partial(attend, own, blocks, heads, lanes),
            name=label("attend", own),
            out_shape=[half_f32, pltpu.VMEM((pairs * HD, HD), BF16)] + last,
            in_specs=[VM] * len(ins),
            out_specs=[VM] * 3,
            scratch_shapes=[] if own else [pltpu.VMEM((C, HD), F32)],
            compiler_params=params(),
            cost_estimate=cost(2 * pairs * narrow, 1 << 20),
        )(*ins)

    def mixing(own, before, attended, q, weighted):
        ins = [docs] + before + [attended, q, weighted]
        outs = [half_bf, states_f32, message] + ([] if own else [column, column])
        return pl.pallas_call(
            functools.partial(mixed, own, blocks, heads, lanes, tp),
            name=label("mixed", own),
            out_shape=outs,
            in_specs=[VM] * len(ins),
            out_specs=[VM] * len(outs),
            scratch_shapes=[] if own else [pltpu.VMEM((HD, C), F32)],
            compiler_params=params(),
            cost_estimate=cost(2 * pairs * narrow, 1 << 20),
        )(*ins)

    def query_grads(own, k, v, q, attended, scale, grad, low, scores, so_far, after):
        ins = [after, k, v, q, attended, scale, gain, grad, low, scores] + list(so_far)
        stage = pltpu.VMEM((blocks, C, cols), BF16)
        return pl.pallas_call(
            functools.partial(query_side, own, blocks, heads),
            name=label("query_side", own),
            out_shape=[whole, whole, half_f32, half_f32, token],
            in_specs=[VM] * 10 + [HB] * len(so_far),
            out_specs=[HB, HB, VM, VM, VM],
            scratch_shapes=[stage, stage, dma((2, blocks))],
            input_output_aliases={10: 0, 11: 1} if own else {},
            compiler_params=params(),
            cost_estimate=cost(8 * pairs * wide, 4 * tokens * cols),
        )(*ins)

    def key_grads(own, inside, carry, k, v, key_local, value_local, so_far):
        ins = [docs, inside, carry, k, v, key_local, value_local] + list(so_far)
        stage = pltpu.VMEM((blocks, C, cols), BF16)
        return pl.pallas_call(
            functools.partial(key_side, own, blocks, heads),
            name=label("key_side", own),
            out_shape=[whole, whole],
            in_specs=[VM] * 7 + [HB] * len(so_far),
            out_specs=[HB, HB],
            scratch_shapes=[stage, stage, dma((2, blocks))],
            input_output_aliases={} if own else {7: 0, 8: 1},
            compiler_params=params(),
            cost_estimate=cost(4 * pairs * narrow, 4 * tokens * cols),
        )(*ins)

    k1, v1, inside1, theirs, docs, k0, v0 = states(False, [])
    v0, inside0, mine = states(True, [k0, v0])
    carry0, carry1, (q1, w1, local1, scores1), (q0, w0, local0, scores0) = scan(
        theirs,
        mine,
        False,
        2,
        lambda after: scoring(False, k1, v1, after),
        lambda after, _: scoring(True, k0, v0, after),
    )
    att0, low0, sums = attending(True, inside0, carry0, q0, local0, w0, None)
    att1, low1, sums = attending(False, inside1, carry1, q1, local1, w1, sums)
    parts = [sums] + [
        lax.ppermute(sums, "tp", [(i, i ^ s) for i in range(tp)]) for s in range(1, tp)
    ]
    grad1, after1, theirs, scale, slope = mixing(False, parts, att1, q1, w1)
    grad0, after0, mine = mixing(True, [scale, slope], att0, q0, w0)
    carry0, carry1, (_, _, kl1, vl1), (normed, query_grad, kl0, vl0) = scan(
        theirs,
        mine,
        True,
        1,
        lambda after: query_grads(False, k1, v1, q1, att1, scale, grad1, low1, scores1, (), after),
        lambda after, done: query_grads(
            True, k0, v0, q0, att0, scale, grad0, low0, scores0, done[:2], after
        ),
    )
    key_grad, value_grad = key_grads(True, after0, carry0, k0, v0, kl0, vl0, ())
    key_grad, value_grad = key_grads(
        False, after1, carry1, k1, v1, kl1, vl1, (key_grad, value_grad)
    )
    return normed, query_grad, key_grad, value_grad


def solution(mesh):
    return jax.shard_map(
        local,
        mesh=mesh,
        in_specs=(
            P("ctx", "tp"),
            P("ctx", "tp"),
            P("ctx", "tp"),
            P("ctx", "tp"),
            P("tp"),
            P("ctx"),
        ),
        out_specs=(P("ctx", "tp"), P("ctx", "tp"), P("ctx", "tp"), P("ctx", "tp")),
        check_vma=False,
    )
```

```python
import functools

import jax
import jax.numpy as jnp
from jax import lax
from jax.experimental import pallas as pl
from jax.experimental.pallas import tpu as pltpu
from jax.sharding import PartitionSpec as P

HD = 128
C = 256
QW = 4096
PAD = 8
NEVER = -1.0e9
MIB = 1 << 20
U_SCORE = 4
U_ATT = 6
U_Q = 6
U_K = 6
T_ATT = 64
T_MIX = 128

epsilon = 1e-06

F32 = jnp.float32
BF16 = jnp.bfloat16
VM = pl.BlockSpec(memory_space=pltpu.VMEM)
HB = pl.BlockSpec(memory_space=pltpu.HBM)


def dot(a, b, dims):
    return lax.dot_general(a, b, (dims, ((), ())), preferred_element_type=F32)


NN = ((1,), (0,))
NT = ((1,), (1,))
TN = ((0,), (0,))


def params(mib=12):
    return pltpu.CompilerParams(vmem_limit_bytes=mib * MIB)


def cost(flops, nbytes):
    return pl.CostEstimate(flops=int(flops), bytes_accessed=int(nbytes), transcendentals=0)


def half_start(own, cols):
    core = lax.rem(lax.axis_index("ctx"), 2)
    half = core if own else 1 - core
    return pl.multiple_of(half * cols, 128)


def label(name, own):
    return name + ("_own" if own else "_other")


def head(h):
    return pl.ds(h * HD, HD)


def block(n):
    return pl.ds(n * C if isinstance(n, int) else pl.multiple_of(n * C, C), C)


def state_rows(n, h, heads):
    start = (n * heads + h) * HD
    return pl.ds(start if isinstance(start, int) else pl.multiple_of(start, HD), HD)


def key_value_states(own, blocks, heads, *refs):
    if own:
        k, _, docs_hbm, v_hbm, v, inside, message, docs, sems = refs
    else:
        docs_hbm, k_hbm, v_hbm, k, v, inside, message, table, k_own, v_own, docs, sems = refs
    off = half_start(own, heads * HD)
    docs_copy = pltpu.make_async_copy(docs_hbm, docs, sems.at[2 * heads])
    width = 2 * HD if heads % 2 == 0 else HD
    groups = heads * HD // width
    copies = [[] for _ in range(groups)]
    for i in range(1 if own else 0, groups):
        src, dst = pl.ds(off + i * width, width), pl.ds(i * width, width)
        copies[i].append(pltpu.make_async_copy(v_hbm.at[:, src], v.at[:, dst], sems.at[2 * i]))
        if not own:
            copies[i].append(
                pltpu.make_async_copy(k_hbm.at[:, src], k.at[:, dst], sems.at[2 * i + 1])
            )
        for copy in copies[i]:
            copy.start()
    docs_copy.start()
    ahead = []
    if not own:
        start = half_start(True, heads * HD)
        ahead = [
            pltpu.make_async_copy(
                k_hbm.at[:, pl.ds(start, heads * HD)], k_own, sems.at[2 * heads + 1]
            ),
            pltpu.make_async_copy(
                v_hbm.at[:, pl.ds(start, width)], v_own.at[:, :width], sems.at[2 * heads + 2]
            ),
        ]
        for copy in ahead:
            copy.start()
    docs_copy.wait()
    for h in range(heads):
        if h * HD % width == 0:
            for copy in copies[h * HD // width]:
                copy.wait()
        per_block = [pl.ds(n * C, C) for n in range(blocks)]
        sums = [dot(k[rows, head(h)], v[rows, head(h)], TN) for rows in per_block]
        running = jnp.zeros((HD, HD), F32)
        for n in range(blocks):
            inside[state_rows(n, h, heads), :] = running
            total = running + sums[n]
            if n + 1 < blocks:
                running = jnp.where(docs[n] == docs[n + 1], total, 0.0)
            else:
                message[head(h), :] = total
    message[heads * HD :, :] = jnp.full((PAD, HD), docs[blocks - 1].astype(F32), F32)
    if not own:
        table[...] = jnp.zeros(table.shape, F32)
        for n in range(blocks):
            table[n : n + 1, :] = jnp.full((1, HD), docs[n].astype(F32), F32)
        for copy in ahead:
            copy.wait()


def causal_mask():
    return lax.broadcasted_iota(jnp.int32, (C, C), 0) >= lax.broadcasted_iota(jnp.int32, (C, C), 1)


def score_rows(n, h, heads):
    start = (n * heads + h) * C
    return pl.ds(start if isinstance(start, int) else pl.multiple_of(start, C), C)


def local_scores(
    own, blocks, heads, after, k, v, gain, q_hbm, g_hbm, q, weighted, local, scores, done, g, sems
):
    off = half_start(own, heads * HD)
    gains = gain[:, pl.ds(off, heads * HD)]
    group = 2 if heads % 2 == 0 else 1
    copies = []
    for h in range(0, heads, group):
        src, dst = pl.ds(off + h * HD, group * HD), pl.ds(h * HD, group * HD)
        copies.append(pltpu.make_async_copy(q_hbm.at[:, src], q.at[:, dst], sems.at[h]))
        copies[-1].start()
    g_copy = pltpu.make_async_copy(g_hbm.at[:, pl.ds(off, heads * HD)], g, sems.at[heads])
    g_copy.start()
    causal = causal_mask()
    for h in range(0, heads, group):
        copies[h // group].wait()
        units = [(n, i) for n in range(blocks) for i in range(h, h + group)]
        for at in range(0, len(units), U_SCORE):
            now = units[at : at + U_SCORE]
            raw = [dot(q[block(n), head(i)], k[block(n), head(i)], NT) for n, i in now]
            low = [jnp.where(causal, s, 0.0).astype(BF16) for s in raw]
            outs = [dot(s, v[block(n), head(i)], NN) for s, (n, i) in zip(low, now)]
            for (n, i), s, out in zip(now, low, outs):
                scores[score_rows(n, i, heads), :] = s
                local[block(n), head(i)] = out
    g_copy.wait()
    for n in range(blocks):
        weighted[block(n), :] = g[block(n), :].astype(F32) * gains
    done[...] = jnp.zeros(done.shape, F32)


def attend(own, blocks, heads, lanes, docs, inside, carry, q, local, weighted, *rest):
    if own:
        attended, low, sums = rest
        sums[...] = jnp.zeros((C, HD), F32)
    else:
        sums_in, attended, low, message, sums = rest
        sums[...] = sums_in[...]
    lane = lax.broadcasted_iota(jnp.int32, (T_ATT, HD), 1)
    every = range(heads)

    def step(n, carried):
        hit = carry[heads * HD : heads * HD + 1, :] == docs[pl.ds(n, 1), :]
        states = []
        for h in every:
            state = inside[state_rows(n, h, heads), :] + jnp.where(hit, carry[head(h), :], 0.0)
            states.append(state.astype(BF16))
            low[state_rows(n, h, heads), :] = states[h]
        for t in range(0, C, T_ATT):
            rows = pl.ds(pl.multiple_of(n * C + t, T_ATT), T_ATT)
            square = jnp.zeros((T_ATT, HD), F32)
            inner = jnp.zeros((T_ATT, HD), F32)
            for h in every:
                out = local[rows, head(h)] + dot(q[rows, head(h)], states[h], NN)
                attended[rows, head(h)] = out
                square += out * out
                inner += weighted[rows, head(h)] * out
            square = jnp.sum(square, axis=1, keepdims=True)
            inner = jnp.sum(inner, axis=1, keepdims=True)
            sums[t : t + T_ATT, :] += jnp.where(lane == n, square, 0.0) + jnp.where(
                lane == n + lanes, inner, 0.0
            )
        return carried

    lax.fori_loop(0, blocks, step, 0, unroll=U_ATT)
    if not own:
        message[...] = jnp.transpose(sums[...])[: 2 * lanes, :]


def mixed(own, blocks, heads, lanes, parts, docs, *rest):
    if not own:
        pieces, rest = rest[:parts], rest[parts:]
        attended, q, weighted, grad, inside, message, scale, slope, turn = rest
        total = pieces[0][...]
        for piece in pieces[1:]:
            total = total + piece[...]
        r = lax.rsqrt(total[:lanes] / QW + epsilon)
        s = r * r * r * (total[lanes:] / QW)
        turn[...] = jnp.zeros((HD, C), F32)
        turn[:lanes, :] = r
        turn[lanes : 2 * lanes, :] = s
        columns = jnp.transpose(turn[...])
        for n in range(blocks):
            rows = pl.ds(n * C, C)
            scale[rows, :] = jnp.broadcast_to(columns[:, n : n + 1], (C, HD))
            slope[rows, :] = jnp.broadcast_to(columns[:, lanes + n : lanes + n + 1], (C, HD))
    else:
        scale, slope, attended, q, weighted, grad, inside, message = rest
    every = range(heads)
    for h in every:
        inside[state_rows(blocks - 1, h, heads), :] = jnp.zeros((HD, HD), F32)
    for n in reversed(range(blocks)):
        rows = pl.ds(n * C, C)
        for t in range(0, C, T_MIX):
            part = pl.ds(n * C + t, T_MIX)
            r = scale[part, :]
            s = slope[part, :]
            for h in every:
                d = r * weighted[part, head(h)] - attended[part, head(h)] * s
                grad[part, head(h)] = d.astype(BF16)
        sums = [dot(q[rows, head(h)], grad[rows, head(h)], TN) for h in every]
        for h in every:
            total = inside[state_rows(n, h, heads), :] + sums[h]
            if n > 0:
                linked = docs[n : n + 1, :] == docs[n - 1 : n, :]
                inside[state_rows(n - 1, h, heads), :] = jnp.where(linked, total, 0.0)
            else:
                message[head(h), :] = total
    message[heads * HD :, :] = jnp.broadcast_to(-docs[0:1, :], (PAD, HD))


def store_blocks(n, slot, pairs, cols, sems):
    return [
        pltpu.make_async_copy(stage.at[slot], out.at[block(n), cols], sems.at[i, slot])
        for i, (stage, out) in enumerate(pairs)
    ]


def query_side(own, blocks, heads, after, k, v, q, attended, scale, gain, grad, low, scores, *rest):
    rest = rest[2:] if own else rest
    normed, query_grad, key_local, value_local, done, stage_n, stage_q, sems = rest
    off = half_start(own, heads * HD)
    cols = pl.ds(off, heads * HD)
    gains = gain[:, cols]
    pairs = ((stage_n, normed), (stage_q, query_grad))
    causal = causal_mask()
    every = range(heads)

    def step(n, carried):
        rows = block(n)
        r = scale[rows, :]
        ds = [grad[rows, head(h)] for h in every]
        raw = [dot(ds[h], v[rows, head(h)], NT) for h in every]
        gs = [jnp.where(causal, x, 0.0).astype(BF16) for x in raw]
        qg = [
            dot(ds[h], low[state_rows(n, h, heads), :], NT) + dot(gs[h], k[rows, head(h)], NN)
            for h in every
        ]
        kg = [dot(q[rows, head(h)], gs[h], TN).T for h in every]
        vg = [dot(ds[h], scores[score_rows(n, h, heads), :], TN).T for h in every]
        outs = [
            attended[rows, head(h)] * r * gains[:, h * HD : (h + 1) * HD] for h in every
        ]
        for h in every:
            stage_q[n, :, head(h)] = qg[h].astype(BF16)
            stage_n[n, :, head(h)] = outs[h].astype(BF16)
            key_local[rows, head(h)] = kg[h]
            value_local[rows, head(h)] = vg[h]
        for copy in store_blocks(n, n, pairs, cols, sems):
            copy.start()
        return carried

    lax.fori_loop(0, blocks, step, 0, unroll=U_Q)
    for n in range(blocks):
        for copy in store_blocks(n, n, pairs, cols, sems):
            copy.wait()
    done[...] = jnp.zeros(done.shape, F32)


def key_side(own, blocks, heads, docs, inside, carry, k, v, key_local, value_local, *rest):
    rest = rest if own else rest[2:]
    key_grad, value_grad, stage_k, stage_v, sems = rest
    off = half_start(own, heads * HD)
    cols = pl.ds(off, heads * HD)
    pairs = ((stage_k, key_grad), (stage_v, value_grad))
    every = range(heads)

    def step(n, carried):
        rows = block(n)
        hit = carry[heads * HD : heads * HD + 1, :] == -docs[pl.ds(n, 1), :]
        states = []
        for h in every:
            state = inside[state_rows(n, h, heads), :] + jnp.where(hit, carry[head(h), :], 0.0)
            states.append(state.astype(BF16))
        key_copy, value_copy = store_blocks(n, n, pairs, cols, sems)
        kg = [dot(v[rows, head(h)], states[h], NT) for h in every]
        for h in every:
            stage_k[n, :, head(h)] = (kg[h] + key_local[rows, head(h)]).astype(BF16)
        key_copy.start()
        vg = [dot(k[rows, head(h)], states[h], NN) for h in every]
        for h in every:
            stage_v[n, :, head(h)] = (vg[h] + value_local[rows, head(h)]).astype(BF16)
        value_copy.start()
        return carried

    lax.fori_loop(0, blocks, step, 0, unroll=U_K)
    for n in range(blocks):
        for copy in store_blocks(n, n, pairs, cols, sems):
            copy.wait()


def merge_kernel(reverse, outs, count, *refs):
    size = lax.axis_size("ctx")
    place = lax.axis_index("ctx")
    rank = size - 1 - place if reverse else place
    core = lax.rem(place, 2)

    def bit(b):
        return lax.rem(lax.div(rank, 1 << b), 2)

    ins, results = refs[:count], refs[count:]
    for pieces, result in zip(outs, results):
        at = 0
        for rows, terms in pieces:
            keys = []
            for source, _, flag in terms:
                end = ins[source].shape[0] - PAD
                key = ins[source][end : end + 1, :]
                keys.append(key if flag is None else jnp.where(flag(bit, core), key, NEVER))
            latest = functools.reduce(jnp.maximum, keys)
            parts = [
                jnp.where(key == latest, ins[source][start : start + rows, :], 0.0)
                for (source, start, _), key in zip(terms, keys)
            ]
            result[at : at + rows, :] = functools.reduce(jnp.add, parts)
            at += rows
        result[at:, :] = jnp.broadcast_to(latest, (PAD, HD))


def merge(ins, outs, reverse, after=()):
    ins = list(ins) + list(after)
    shapes = [pltpu.VMEM((sum(rows for rows, _ in pieces) + PAD, HD), F32) for pieces in outs]
    return pl.pallas_call(
        functools.partial(merge_kernel, reverse, outs, len(ins)),
        name="merge",
        out_shape=shapes,
        in_specs=[VM] * len(ins),
        out_specs=[VM] * len(outs),
        compiler_params=params(),
        cost_estimate=cost(0, 1 << 18),
    )(*ins)


def swap(message, even, odd):
    size = lax.axis_size("ctx")
    pairs = [(i, i ^ (1 << (odd if i % 2 else even))) for i in range(size)]
    return lax.ppermute(message, "ctx", pairs)


def scan(theirs, mine, reverse, ways, first_work, second_work):
    rows = mine.shape[0] - PAD
    part = rows // ways
    every = range(ways)
    top = lax.axis_size("ctx").bit_length() - 1
    lo, hi = top - 2, top - 1

    def routed(way, flag):
        return lambda bit, core: flag(bit(lo), bit(hi), core if ways == 1 else way)

    def axes(way):
        return (lo, hi) if ways == 1 else ((lo, lo), (hi, hi))[way]

    beside = swap(theirs, 0, 0)
    totals = merge(
        [mine, beside],
        [[(part, [(0, w * part, None), (1, w * part, None)])] for w in every],
        reverse,
    )
    before = []
    for b in range(1, lo):
        got = [swap(totals[w], b, b) for w in every]

        def is_high(bit, core, b=b):
            return bit(b) == 1

        earlier = [[(2 * ways + w, 0, None)] if before else [] for w in every]
        both = merge(
            list(totals) + got + list(before),
            [[(part, [(w, 0, None), (ways + w, 0, None)])] for w in every]
            + [[(part, [(ways + w, 0, is_high)] + earlier[w])] for w in every],
            reverse,
        )
        totals, before = both[:ways], both[ways:]
    first = [swap(totals[w], *axes(w)) for w in every]
    first_done = first_work(totals[0])
    onward = [
        merge(
            [totals[w], first[w]],
            [
                [
                    (
                        part,
                        [
                            (0, 0, routed(w, lambda low, high, r: r * low * high == 0)),
                            (1, 0, routed(w, lambda low, high, r: r * (1 - high) == 0)),
                        ],
                    )
                ]
            ],
            reverse,
            first_done[-1:],
        )[0]
        for w in every
    ]
    second = [swap(onward[w], *axes(w)[::-1] if ways == 1 else axes(1 - w)) for w in every]
    second_done = second_work(onward[-1], first_done)

    def carried(neighbour, low_core):
        return [
            (
                part,
                [
                    (w, 0, routed(w, lambda low, high, r: (1 - r) * low + r * high == 1)),
                    (ways + w, 0, routed(w, lambda low, high, r: high + r * low > 0)),
                    (neighbour, w * part, lambda bit, core: bit(0) == low_core),
                ]
                + ([(2 * ways + 2 + w, 0, None)] if before else []),
            )
            for w in every
        ]

    carry_mine, carry_theirs = merge(
        first + second + [beside, mine] + list(before),
        [carried(2 * ways, 1), carried(2 * ways + 1, 0)],
        reverse,
        second_done[-1:],
    )
    return carry_mine, swap(carry_theirs, 0, 0), first_done[:-1], second_done[:-1]


def local(queries, keys, values, out_grad, gain, doc_ids):
    tokens, features = queries.shape
    heads = features // HD // 2
    cols = heads * HD
    blocks = tokens // C
    lanes = -(-blocks // 8) * 8
    pairs = blocks * heads
    tp = lax.axis_size("tp")
    gain = gain.reshape(1, features)
    rows = cols + PAD
    narrow, wide, square = C * HD * HD, C * C * HD, HD * HD
    dma = pltpu.SemaphoreType.DMA
    half_bf = pltpu.VMEM((tokens, cols), BF16)
    half_f32 = pltpu.VMEM((tokens, cols), F32)
    states_f32 = pltpu.VMEM((pairs * HD, HD), F32)
    message = pltpu.VMEM((rows, HD), F32)
    whole = pltpu.HBM((tokens, features), BF16)
    column = pltpu.VMEM((tokens, HD), F32)

    keys, values, queries, out_grad, docs_hbm = [
        pltpu.with_memory_space_constraint(x, pltpu.HBM)
        for x in (keys, values, queries, out_grad, doc_ids)
    ]
    token = pltpu.VMEM((PAD, HD), F32)

    def states(own, ahead):
        ins = ahead + ([docs_hbm, values] if own else [docs_hbm, keys, values])
        outs = [half_bf, states_f32, message]
        if not own:
            outs = [half_bf] + outs + [pltpu.VMEM((lanes, HD), F32), half_bf, half_bf]
        return pl.pallas_call(
            functools.partial(key_value_states, own, blocks, heads),
            name=label("states", own),
            out_shape=outs,
            in_specs=[VM] * len(ahead) + [HB] * (len(ins) - len(ahead)),
            out_specs=[VM] * len(outs),
            scratch_shapes=[pltpu.SMEM((blocks,), jnp.int32), dma((2 * heads + 3,))],
            input_output_aliases={1: 0} if own else {},
            compiler_params=params(),
            cost_estimate=cost(2 * pairs * narrow, 4 * tokens * cols),
        )(*ins)

    def scoring(own, k, v, after):
        return pl.pallas_call(
            functools.partial(local_scores, own, blocks, heads),
            name=label("scoring", own),
            out_shape=[half_bf, half_f32, half_f32, pltpu.VMEM((pairs * C, C), BF16), token],
            in_specs=[VM] * 4 + [HB] * 2,
            out_specs=[VM] * 5,
            scratch_shapes=[half_bf, dma((heads + 1,))],
            compiler_params=params(),
            cost_estimate=cost(4 * pairs * wide, 4 * tokens * cols),
        )(after, k, v, gain, queries, out_grad)

    def attending(own, inside, carry, q, sv, weighted, sums):
        ins = [docs, inside, carry, q, sv, weighted] + ([] if own else [sums])
        last = [pltpu.VMEM((C, HD), F32)] if own else [pltpu.VMEM((2 * lanes, C), F32)]
        return pl.pallas_call(
            functools.partial(attend, own, blocks, heads, lanes),
            name=label("attend", own),
            out_shape=[half_f32, pltpu.VMEM((pairs * HD, HD), BF16)] + last,
            in_specs=[VM] * len(ins),
            out_specs=[VM] * 3,
            scratch_shapes=[] if own else [pltpu.VMEM((C, HD), F32)],
            compiler_params=params(),
            cost_estimate=cost(2 * pairs * narrow, 1 << 20),
        )(*ins)

    def mixing(own, before, attended, q, weighted):
        ins = [docs] + before + [attended, q, weighted]
        outs = [half_bf, states_f32, message] + ([] if own else [column, column])
        return pl.pallas_call(
            functools.partial(mixed, own, blocks, heads, lanes, tp),
            name=label("mixed", own),
            out_shape=outs,
            in_specs=[VM] * len(ins),
            out_specs=[VM] * len(outs),
            scratch_shapes=[] if own else [pltpu.VMEM((HD, C), F32)],
            compiler_params=params(),
            cost_estimate=cost(2 * pairs * narrow, 1 << 20),
        )(*ins)

    def query_grads(own, k, v, q, attended, scale, grad, low, scores, so_far, after):
        ins = [after, k, v, q, attended, scale, gain, grad, low, scores] + list(so_far)
        stage = pltpu.VMEM((blocks, C, cols), BF16)
        return pl.pallas_call(
            functools.partial(query_side, own, blocks, heads),
            name=label("query_side", own),
            out_shape=[whole, whole, half_f32, half_f32, token],
            in_specs=[VM] * 10 + [HB] * len(so_far),
            out_specs=[HB, HB, VM, VM, VM],
            scratch_shapes=[stage, stage, dma((2, blocks))],
            input_output_aliases={10: 0, 11: 1} if own else {},
            compiler_params=params(),
            cost_estimate=cost(8 * pairs * wide, 4 * tokens * cols),
        )(*ins)

    def key_grads(own, inside, carry, k, v, key_local, value_local, so_far):
        ins = [docs, inside, carry, k, v, key_local, value_local] + list(so_far)
        stage = pltpu.VMEM((blocks, C, cols), BF16)
        return pl.pallas_call(
            functools.partial(key_side, own, blocks, heads),
            name=label("key_side", own),
            out_shape=[whole, whole],
            in_specs=[VM] * 7 + [HB] * len(so_far),
            out_specs=[HB, HB],
            scratch_shapes=[stage, stage, dma((2, blocks))],
            input_output_aliases={} if own else {7: 0, 8: 1},
            compiler_params=params(),
            cost_estimate=cost(4 * pairs * narrow, 4 * tokens * cols),
        )(*ins)

    k1, v1, inside1, theirs, docs, k0, v0 = states(False, [])
    v0, inside0, mine = states(True, [k0, v0])
    carry0, carry1, (q1, w1, local1, scores1), (q0, w0, local0, scores0) = scan(
        theirs,
        mine,
        False,
        2,
        lambda after: scoring(False, k1, v1, after),
        lambda after, _: scoring(True, k0, v0, after),
    )
    att0, low0, sums = attending(True, inside0, carry0, q0, local0, w0, None)
    att1, low1, sums = attending(False, inside1, carry1, q1, local1, w1, sums)
    parts = [sums] + [
        lax.ppermute(sums, "tp", [(i, i ^ s) for i in range(tp)]) for s in range(1, tp)
    ]
    grad1, after1, theirs, scale, slope = mixing(False, parts, att1, q1, w1)
    grad0, after0, mine = mixing(True, [scale, slope], att0, q0, w0)
    carry0, carry1, (_, _, kl1, vl1), (normed, query_grad, kl0, vl0) = scan(
        theirs,
        mine,
        True,
        1,
        lambda after: query_grads(False, k1, v1, q1, att1, scale, grad1, low1, scores1, (), after),
        lambda after, done: query_grads(
            True, k0, v0, q0, att0, scale, grad0, low0, scores0, done[:2], after
        ),
    )
    key_grad, value_grad = key_grads(True, after0, carry0, k0, v0, kl0, vl0, ())
    key_grad, value_grad = key_grads(
        False, after1, carry1, k1, v1, kl1, vl1, (key_grad, value_grad)
    )
    return normed, query_grad, key_grad, value_grad


def solution(mesh):
    return jax.shard_map(
        local,
        mesh=mesh,
        in_specs=(
            P("ctx", "tp"),
            P("ctx", "tp"),
            P("ctx", "tp"),
            P("ctx", "tp"),
            P("tp"),
            P("ctx"),
        ),
        out_specs=(P("ctx", "tp"), P("ctx", "tp"), P("ctx", "tp"), P("ctx", "tp")),
        check_vma=False,
    )
```
